256 devices in a mesh: ctx: 128 (over z, x, y), ch: 2 (over core).
Axes of the slice: x: 4, y: 4, z: 8, core: 2. Of those that a mesh axis runs over, the one named last changes fastest.
Arguments:
- query_in: bfloat16 [16384, 2048], P('ctx', 'ch'), may hold values from -6 to 6
- key_in: bfloat16 [16384, 2048], P('ctx', 'ch'), may hold values from -6 to 6
- value_in: bfloat16 [16384, 2048], P('ctx', 'ch'), may hold values from -6 to 6
- taps: float32 [3, 7, 2048], P(None, None, 'ch'), may hold values from -2 to 2
- long_filter: float32 [16384, 2048], P('ctx', 'ch'), may hold values from -181.01934 to 181.01934
- out_weight: bfloat16 [2048, 2048], P('ch'), may hold values from -0.125 to 0.125
- out_grad: bfloat16 [16384, 2048], P('ctx', 'ch'), may hold values from -6 to 6
Outputs:
- block_out: bfloat16 [16384, 2048], P('ctx', 'ch')
- grad_query: bfloat16 [16384, 2048], P('ctx', 'ch')
- grad_key: bfloat16 [16384, 2048], P('ctx', 'ch')
- grad_value: bfloat16 [16384, 2048], P('ctx', 'ch')
- grad_filter: float32 [16384, 2048], P('ctx', 'ch')
The draws below stay inside these ranges and needn't reach their ends.
All inputs are finite; a program needn't handle non-finite values.
Results may differ from the reference program's by a relative error of at most 0.0049.
Values may be sent and summed in bfloat16 or wider, within the bound.
No kernel may reach another device: no remote copies, remote signals or barrier semaphores. Data moves between devices by JAX's collectives and lax.ppermute only.
A program may use at most 128 MiB of HBM per device.

```python
import math
import jax
import jax.numpy as jnp

D = 2048
TAPS = 7
SEQ = 16384


def draw_long_filter(key, part):
    key = jax.random.fold_in(key, 17)
    rate_key, rough_key = jax.random.split(key)
    positions = jnp.arange(SEQ, dtype=jnp.float32)[:, None]
    spans = jnp.exp(jax.random.uniform(rate_key, (D,), jnp.float32, math.log(16.0), math.log(256.0 * SEQ)))
    rough = jnp.clip(jax.random.normal(rough_key, (SEQ, D), jnp.float32), -4.0, 4.0)
    keep = jnp.sqrt(2.0 * SEQ / jnp.minimum(spans, 1.0 * SEQ))
    return (rough * jnp.exp(-positions / spans[None, :]) * keep[None, :]).astype(jnp.float32)


def level_of(stream_key, dims, cuts, smallest, high):
    factor_of = 1.0
    for position, blocks in cuts:
        draws = jax.random.uniform(jax.random.fold_in(jax.random.fold_in(stream_key, 6), position), (blocks,), jnp.float32, smallest / len(cuts), high / len(cuts))
        factor_of = factor_of * jnp.repeat(jnp.exp(draws), dims[position] // blocks).reshape((-1,) + (1,) * (len(dims) - 1 - position))
    return factor_of


def centred(own_key, shape, deviation, limit, cuts=(), kind=jnp.bfloat16):
    loudness = level_of(own_key, shape, cuts, -0.22, 0.18) if cuts else 1.0
    drawn = jax.random.normal(own_key, shape, jnp.float32) * deviation * loudness
    return jnp.minimum(jnp.maximum(drawn, -limit), limit).astype(kind)


def setup_inputs(seed: int = 0) -> dict:
    keys = jax.random.split(jax.random.key(seed), 8)
    query_in = centred(keys[0], (SEQ, D), 1.0, 6.0, ((0, 128), (1, 2)))
    key_in = centred(keys[1], (SEQ, D), 1.0, 6.0, ((0, 128), (1, 2)))
    value_in = centred(keys[2], (SEQ, D), 1.0, 6.0, ((0, 128), (1, 2)))
    taps = centred(keys[3], (3, TAPS, D), TAPS ** -0.5, 2.0, ((2, 2),), jnp.float32)
    long_filter = draw_long_filter(jax.random.fold_in(keys[7], 71), 0)
    out_weight = centred(keys[5], (D, D), D ** -0.5, 0.125, ((0, 2),))
    out_grad = centred(keys[6], (SEQ, D), 1.0, 6.0, ((0, 128), (1, 2)))
    return {"query_in": query_in, "key_in": key_in, "value_in": value_in, "taps": taps, "long_filter": long_filter, "out_weight": out_weight, "out_grad": out_grad}


def short_conv(values, taps_row):
    padded = jnp.pad(values, ((TAPS - 1, 0), (0, 0)))
    total = jnp.zeros(values.shape, jnp.float32)
    for shift in range(TAPS):
        start = TAPS - 1 - shift
        total = total + taps_row[shift] * padded[start:start + SEQ]
    return total

def short_back(values, taps_row):
    padded = jnp.pad(values, ((0, TAPS - 1), (0, 0)))
    total = jnp.zeros(values.shape, jnp.float32)
    for shift in range(TAPS):
        total = total + taps_row[shift] * padded[shift:shift + SEQ]
    return total

def forward_spec(values):
    return jnp.fft.rfft(values, n=2 * SEQ, axis=0)

def inverse_spec(values):
    return jnp.fft.irfft(values, n=2 * SEQ, axis=0)[:SEQ]

def reference(query_in, key_in, value_in, taps, long_filter, out_weight, out_grad):
    q_short = short_conv(query_in.astype(jnp.float32), taps[0])
    k_short = short_conv(key_in.astype(jnp.float32), taps[1])
    v_short = short_conv(value_in.astype(jnp.float32), taps[2])
    mixed = k_short * v_short
    scale = 1.0 / math.sqrt(SEQ)
    kernel = long_filter * scale
    mixed_spec = forward_spec(mixed)
    kernel_spec = forward_spec(kernel)
    long_out = inverse_spec(mixed_spec * kernel_spec)
    gated = (q_short * long_out).astype(jnp.bfloat16)
    block_out = jnp.dot(gated, out_weight, preferred_element_type=jnp.float32).astype(jnp.bfloat16)
    grad_gated = jnp.dot(out_grad, out_weight.T, preferred_element_type=jnp.float32)
    grad_qs = grad_gated * long_out
    grad_long = grad_gated * q_short
    long_spec = forward_spec(grad_long)
    grad_mixed = inverse_spec(jnp.conj(kernel_spec) * long_spec)
    grad_filter = inverse_spec(jnp.conj(mixed_spec) * long_spec) * scale
    grad_ks = grad_mixed * v_short
    grad_vs = grad_mixed * k_short
    grad_query = short_back(grad_qs, taps[0]).astype(jnp.bfloat16)
    grad_key = short_back(grad_ks, taps[1]).astype(jnp.bfloat16)
    grad_value = short_back(grad_vs, taps[2]).astype(jnp.bfloat16)
    return (block_out, grad_query, grad_key, grad_value, grad_filter)
```

```python
import math

import jax
import jax.numpy as jnp
import ml_dtypes
import numpy as np
from jax import lax
from jax.experimental import pallas as pl
from jax.experimental.pallas import tpu as pltpu
from jax.sharding import PartitionSpec as P

f32 = jnp.float32
bf16 = jnp.bfloat16
EDGE = 8
WIDE = 256
VMEM_LIMIT = 48 * 1024 * 1024


def shifted(value, axis, steps):
    count = lax.axis_size(axis)
    first, last = (max(0, -steps), min(count, count - steps))
    return lax.ppermute(value, axis, [(source, source + steps) for source in range(first, last)])


def halves(table):
    high = table.astype(ml_dtypes.bfloat16)
    low = (table - high.astype(np.float64)).astype(ml_dtypes.bfloat16)
    return high, low


def tables(parts, rows, gain):
    freqs = np.arange(parts) + 0.5
    blocks = np.arange(parts)
    inner = np.arange(rows)
    outer = np.outer(freqs, blocks) * (-2.0 * math.pi / (2 * parts))
    turn = np.outer(freqs, inner) * (-2.0 * math.pi / (2 * parts * rows))
    small = np.outer(inner, inner) % rows * (-2.0 * math.pi / rows)
    first = halves(np.concatenate([np.cos(outer), np.sin(outer)], 0))
    first = np.concatenate(first, 1)
    c, s = np.cos(small), np.sin(small)
    high, low = halves(np.block([[c, s], [-s, c]]))
    second = np.concatenate([high, high, low], 0)
    high, low = halves(np.block([[c, -s], [s, c]]))
    back = np.concatenate([high, high, low], 0)
    high, low = halves(np.concatenate([np.cos(outer).T, np.sin(outer).T], 1) * gain)
    last = np.concatenate([high, high, low], 1)
    twist = np.stack([np.cos(turn), np.sin(turn)]).astype(np.float32)
    return first, second, back, last, twist


def split(value):
    high = value.astype(bf16)
    low = (value - high.astype(f32)).astype(bf16)
    return high, low


def prepare_kernel(q, k, v, halo, taps, filt, mine, other, w_mine, w_other, send, qs, ks, vs, gg, pad):
    rows, width = q.shape

    def short(x, which):
        pad[0:EDGE, :] = halo[which].astype(f32)
        pad[EDGE : EDGE + rows, :] = x[...].astype(f32)
        total = taps[which, 0:1, :] * pad[EDGE : EDGE + rows, :]
        for shift in range(1, taps.shape[1]):
            total = total + taps[which, shift : shift + 1, :] * pad[EDGE - shift : EDGE - shift + rows, :]
        return total

    across = (((1,), (1,)), ((), ()))
    grad = lax.dot_general(mine[...], w_mine[...], across, preferred_element_type=f32)
    grad = grad + lax.dot_general(other[...], w_other[...], across, preferred_element_type=f32)
    gg[...] = grad
    q_short = short(q, 0)
    qs[...] = q_short
    k_short = short(k, 1)
    ks[...] = k_short
    v_short = short(v, 2)
    vs[...] = v_short
    fields = (k_short * v_short, filt[...], grad * q_short)
    turned = [field.T.reshape(width // 8, 8, rows) for field in fields]
    send[...] = jnp.concatenate(turned, axis=1).astype(bf16)


def spectral_kernel(x, first, second, back, last, twist, out, buf):
    parts, lines, rows = x.shape
    group = lines // 3
    buf[...] = x[...].astype(f32).reshape(parts * lines, rows)
    cos, sin = twist[0], twist[1]

    def dot(left, right):
        return jnp.dot(left, right, preferred_element_type=f32)

    def wide(value, table):
        high, low = split(value)
        return dot(jnp.concatenate([high, low, high], 1), table[...])

    for c in range(group):
        places = [pl.ds(f * group + c, parts, stride=lines) for f in range(3)]
        field = jnp.concatenate([buf[place, :] for place in places], 1).astype(bf16)
        half = dot(first[...], jnp.concatenate([field, field], 0))
        turned = []
        for f in range(3):
            re = half[:parts, f * rows : (f + 1) * rows]
            im = half[parts:, f * rows : (f + 1) * rows]
            turned.append(jnp.concatenate([re * cos - im * sin, re * sin + im * cos], 1))
        spec = wide(jnp.concatenate(turned, 0), second)
        (xr, xi), (kr, ki), (gr, gi) = [
            (spec[f * parts : (f + 1) * parts, :rows], spec[f * parts : (f + 1) * parts, rows:])
            for f in range(3)
        ]
        long_spec = jnp.concatenate([xr * kr - xi * ki, xr * ki + xi * kr], 1)
        mixed_spec = jnp.concatenate([kr * gr + ki * gi, kr * gi - ki * gr], 1)
        filter_spec = jnp.concatenate([xr * gr + xi * gi, xr * gi - xi * gr], 1)
        part = wide(jnp.concatenate([long_spec, mixed_spec, filter_spec], 0), back)
        turned = []
        for f in range(3):
            re = part[f * parts : (f + 1) * parts, :rows]
            im = part[f * parts : (f + 1) * parts, rows:]
            turned.append(jnp.concatenate([re * cos + im * sin, im * cos - re * sin], 0))
        high, low = split(jnp.concatenate(turned, 1))
        result = dot(last[...], jnp.concatenate([high, low, high], 0))
        for f in range(3):
            buf[places[f], :] = result[:, f * rows : (f + 1) * rows]
    out[...] = buf[...].reshape(parts, lines, rows).astype(bf16)


def finish_kernel(here, landed, qs, ks, vs, gg, w_mine, w_other, gq, gk, gv, gf, heads, mine, other, total):
    step = pl.program_id(0)
    count, lines, rows = landed.shape
    group = lines // 3
    values = landed[...].astype(f32)
    long_out, grad_mixed, grad_filter = [
        values[:, f * group : (f + 1) * group, :].reshape(count * group, rows).T for f in range(3)
    ]
    gated = (qs[...] * long_out).astype(bf16)
    mine_part = jnp.dot(gated, w_mine[...], preferred_element_type=f32)
    other_part = jnp.dot(gated, w_other[...], preferred_element_type=f32)

    @pl.when(step == 0)
    def _():
        mine[...] = mine_part
        total[...] = other_part

    @pl.when(step > 0)
    def _():
        mine[...] += mine_part
        total[...] += other_part

    other[...] = total[...].astype(bf16)
    gf[...] = grad_filter
    for which, (to, value) in enumerate(
        ((gq, gg[...] * long_out), (gk, grad_mixed * vs[...]), (gv, grad_mixed * ks[...]))
    ):
        to[...] = value
        heads[which] = value[:EDGE, :].astype(bf16)


def close_kernel(gq, gk, gv, after, taps, mine, other, block_out, oq, ok, ov, pad):
    rows, width = gq.shape
    for which, (value, to) in enumerate(((gq, oq), (gk, ok), (gv, ov))):
        pad[0:rows, :] = value[...]
        pad[rows : rows + EDGE, :] = after[which].astype(f32)
        total = taps[which, 0:1, :] * pad[0:rows, :]
        for shift in range(1, taps.shape[1]):
            total = total + taps[which, shift : shift + 1, :] * pad[shift : shift + rows, :]
        to[...] = total.astype(bf16)
    block_out[...] = (mine[...] + other[...].astype(f32)).astype(bf16)


def on_device(query_in, key_in, value_in, taps, long_filter, out_weight, out_grad):
    rows, width = query_in.shape
    parts = lax.axis_size("ctx")
    seq_total = parts * rows
    group = width // parts
    lines = 3 * group
    reach = taps.shape[1]
    outs = out_weight.shape[1]
    here = lax.axis_index("ch").astype(jnp.int32).reshape(1)
    gain = 1.0 / math.sqrt(seq_total) / seq_total
    swap = [(0, 1), (1, 0)]

    tails = jnp.stack([query_in[rows - EDGE :], key_in[rows - EDGE :], value_in[rows - EDGE :]])
    halo = shifted(tails, "ctx", 1)
    grad_other = lax.ppermute(out_grad, "ch", swap)

    steps = width // WIDE
    column = pl.BlockSpec((rows, WIDE), lambda i, me: (0, i))
    edge = pl.BlockSpec((3, EDGE, WIDE), lambda i, me: (0, 0, i))
    taps_spec = pl.BlockSpec((3, reach, WIDE), lambda i, me: (0, 0, i))
    whole = pl.BlockSpec((rows, width), lambda i, me: (0, 0))
    w_mine = pl.BlockSpec((WIDE, outs // 2), lambda i, me: (i, me[0]))
    w_other = pl.BlockSpec((WIDE, outs // 2), lambda i, me: (i, 1 - me[0]))
    chunk = pl.BlockSpec((WIDE // group, lines, rows), lambda i, me: (i, 0, 0))
    params = pltpu.CompilerParams(vmem_limit_bytes=VMEM_LIMIT)
    flat = jax.ShapeDtypeStruct((rows, width), f32)
    half = jax.ShapeDtypeStruct((rows, width), bf16)
    fields = jax.ShapeDtypeStruct((parts, lines, rows), bf16)

    with jax.named_scope("prepare"):
        send, qs, ks, vs, gg = pl.pallas_call(
            prepare_kernel_with_index,
            grid_spec=pltpu.PrefetchScalarGridSpec(
                num_scalar_prefetch=1,
                grid=(steps,),
                in_specs=[column] * 3 + [edge, taps_spec, column, whole, whole, w_mine, w_other],
                out_specs=[chunk] + [column] * 4,
                scratch_shapes=[pltpu.VMEM((rows + EDGE, WIDE), f32)],
            ),
            out_shape=[fields, flat, flat, flat, flat],
            compiler_params=params,
        )(here, query_in, key_in, value_in, halo, taps, long_filter, out_grad, grad_other, out_weight, out_weight)

    arrived = lax.all_to_all(send, "ctx", split_axis=0, concat_axis=0, tiled=True)

    with jax.named_scope("spectral"):
        solved = pl.pallas_call(
            spectral_kernel,
            out_shape=fields,
            scratch_shapes=[pltpu.VMEM((parts * lines, rows), f32)],
            compiler_params=params,
        )(arrived, *tables(parts, rows, gain))

    landed = lax.all_to_all(solved, "ctx", split_axis=0, concat_axis=0, tiled=True)

    with jax.named_scope("finish"):
        gq, gk, gv, grad_filter, heads, mine, other = pl.pallas_call(
            finish_kernel,
            grid_spec=pltpu.PrefetchScalarGridSpec(
                num_scalar_prefetch=1,
                grid=(steps,),
                in_specs=[chunk] + [column] * 4 + [w_mine, w_other],
                out_specs=[column] * 4 + [edge, whole, whole],
                scratch_shapes=[pltpu.VMEM((rows, width), f32)],
            ),
            out_shape=[flat] * 4 + [jax.ShapeDtypeStruct((3, EDGE, width), bf16), flat, half],
            compiler_params=params,
        )(here, landed, qs, ks, vs, gg, out_weight, out_weight)

    theirs = lax.ppermute(other, "ch", swap)
    after = shifted(heads, "ctx", -1)

    with jax.named_scope("close"):
        column = pl.BlockSpec((rows, WIDE), lambda i: (0, i))
        edge = pl.BlockSpec((3, EDGE, WIDE), lambda i: (0, 0, i))
        taps_spec = pl.BlockSpec((3, reach, WIDE), lambda i: (0, 0, i))
        block_out, grad_query, grad_key, grad_value = pl.pallas_call(
            close_kernel,
            grid=(steps,),
            in_specs=[column] * 3 + [edge, taps_spec, column, column],
            out_specs=[column] * 4,
            out_shape=[half] * 4,
            scratch_shapes=[pltpu.VMEM((rows + EDGE, WIDE), f32)],
            compiler_params=params,
        )(gq, gk, gv, after, taps, mine, theirs)
    return (block_out, grad_query, grad_key, grad_value, grad_filter)


def prepare_kernel_with_index(here, *refs):
    prepare_kernel(*refs)


def solution(mesh):
    return jax.shard_map(
        on_device,
        mesh=mesh,
        in_specs=(
            P("ctx", "ch"),
            P("ctx", "ch"),
            P("ctx", "ch"),
            P(None, None, "ch"),
            P("ctx", "ch"),
            P("ch", None),
            P("ctx", "ch"),
        ),
        out_specs=(P("ctx", "ch"), P("ctx", "ch"), P("ctx", "ch"), P("ctx", "ch"), P("ctx", "ch")),
        check_vma=False,
    )
```

```python
import math

import jax
import jax.numpy as jnp
import ml_dtypes
import numpy as np
from jax import lax
from jax.experimental import pallas as pl
from jax.experimental.pallas import tpu as pltpu
from jax.sharding import PartitionSpec as P

f32 = jnp.float32
bf16 = jnp.bfloat16
EDGE = 8
TAIL = 16
WIDE = 256
VMEM_LIMIT = 24 * 1024 * 1024


def shifted(value, axis, steps):
    count = lax.axis_size(axis)
    first, last = (max(0, -steps), min(count, count - steps))
    return lax.ppermute(value, axis, [(source, source + steps) for source in range(first, last)])


def halves(table):
    high = table.astype(ml_dtypes.bfloat16)
    low = (table - high.astype(np.float64)).astype(ml_dtypes.bfloat16)
    return high, low


def ring_order(parts):
    length = math.gcd(parts, 8)
    ring = [place for place in (3, 1, 2, 7, 6, 0, 5, 4) if place < length]
    plane = parts // length
    return [place * plane + spot for spot in range(plane) for place in ring]


def tables(parts, rows, gain, order):
    freqs = np.arange(parts) + 0.5
    blocks = np.asarray(order)
    inner = np.arange(rows)
    outer = np.outer(freqs, blocks) * (-2.0 * math.pi / (2 * parts))
    turn = np.outer(freqs, inner) * (-2.0 * math.pi / (2 * parts * rows))
    small = np.outer(inner, inner) % rows * (-2.0 * math.pi / rows)
    first = halves(np.concatenate([np.cos(outer), np.sin(outer)], 0))
    first = np.concatenate(first, 1)
    c, s = np.cos(small), np.sin(small)
    high, low = halves(np.block([[c, s], [-s, c]]))
    second = np.concatenate([high, high, low], 0)
    high, low = halves(np.block([[c, -s], [s, c]]))
    back = np.concatenate([high, high, low], 0)
    high, low = halves(np.concatenate([np.cos(outer).T, np.sin(outer).T], 1) * gain)
    last = np.concatenate([high, high, low], 1)
    twist = np.stack([np.cos(turn), np.sin(turn)]).astype(np.float32)
    return first, second, back, last, twist


def split(value):
    high = value.astype(bf16)
    low = (value - high.astype(f32)).astype(bf16)
    return high, low


def tails_kernel(q, k, v, out, sems):
    rows = q.shape[0]
    copies = [
        pltpu.make_async_copy(x.at[pl.ds(rows - TAIL, TAIL), :], out.at[which], sems.at[which])
        for which, x in enumerate((q, k, v))
    ]
    for copy in copies:
        copy.start()
    for copy in copies:
        copy.wait()


ACROSS = (((1,), (1,)), ((), ()))


def fetch_kernel(
    here, q, k, v, filt, mine, w, taps_in, qs, ks, vs, gg, ft, wm, wo, taps, qb, kb, vb, fb, mb, pad, sems
):
    rows, width = q.shape
    half = w.shape[1] // 2
    me = here[0]
    w_mine = w.at[:, pl.ds(pl.multiple_of(me * half, half), half)]
    w_other = w.at[:, pl.ds(pl.multiple_of((1 - me) * half, half), half)]
    pairs = ((taps_in, taps), (q, qb), (k, kb), (v, vb), (filt, fb), (mine, mb), (w_mine, wm), (w_other, wo))
    copies = [pltpu.make_async_copy(src, dst, sems.at[i]) for i, (src, dst) in enumerate(pairs)]
    for copy in copies:
        copy.start()
    pad[0:EDGE, :] = jnp.zeros((EDGE, WIDE), f32)
    copies[0].wait()
    for which, (buf, out) in enumerate(((qb, qs), (kb, ks), (vb, vs))):
        copies[1 + which].wait()
        for first in range(0, width, WIDE):
            columns = slice(first, first + WIDE)
            pad[EDGE : EDGE + rows, :] = buf[:, columns].astype(f32)
            total = taps[which, 0:1, columns] * pad[EDGE : EDGE + rows, :]
            for shift in range(1, taps.shape[1]):
                moved = pad[EDGE - shift : EDGE - shift + rows, :]
                total = total + taps[which, shift : shift + 1, columns] * moved
            out[:, columns] = total
    copies[4].wait()
    for first in range(0, width, WIDE):
        ft[first : first + WIDE, :] = fb[:, first : first + WIDE].T
    copies[5].wait()
    copies[6].wait()
    for first in range(0, width, WIDE):
        part = slice(first, first + WIDE)
        gg[:, part] = lax.dot_general(mb[...], wm[part, :], ACROSS, preferred_element_type=f32)
    copies[7].wait()


def prepare_kernel(halo, taps, qs_in, ks_in, vs_in, gg_in, ft, other, wo, send, qs, ks, vs, gg, pad):
    rows, width = gg.shape
    parts, lines, _ = send.shape
    group = lines // 3
    pad[EDGE : 2 * EDGE, :] = jnp.zeros((EDGE, WIDE), f32)
    for first in range(0, width, WIDE):
        part = slice(first, first + WIDE)
        grad = gg_in[:, part] + lax.dot_general(other[...], wo[part, :], ACROSS, preferred_element_type=f32)
        gg[:, part] = grad
        shorts = []
        for which, (before, after) in enumerate(((qs_in, qs), (ks_in, ks), (vs_in, vs))):
            pad[0:EDGE, :] = halo[which, :, part].astype(f32)[TAIL - EDGE :, :]
            top = before[0:EDGE, part]
            for shift in range(1, taps.shape[1]):
                top = top + taps[which, shift : shift + 1, part] * pad[EDGE - shift : 2 * EDGE - shift, :]
            value = jnp.concatenate([top, before[EDGE:, part]], 0)
            after[:, part] = value
            shorts.append(value)
        mixed = (shorts[1] * shorts[2]).T
        grad_long = (grad * shorts[0]).T
        turned = [field.reshape(WIDE // group, group, rows) for field in (mixed, ft[part, :], grad_long)]
        send[first // group : (first + WIDE) // group] = jnp.concatenate(turned, axis=1).astype(bf16)


def spectral_kernel(x, first, second, back, last, twist, out, buf):
    parts, lines, rows = x.shape
    group = lines // 3
    buf[...] = x[...].astype(f32).reshape(parts * lines, rows)
    cos, sin = twist[0], twist[1]

    def dot(left, right):
        return jnp.dot(left, right, preferred_element_type=f32)

    def wide(value, table):
        high, low = split(value)
        return dot(jnp.concatenate([high, low, high], 1), table[...])

    for c in range(group):
        places = [pl.ds(f * group + c, parts, stride=lines) for f in range(3)]
        field = jnp.concatenate([buf[place, :] for place in places], 1).astype(bf16)
        half = dot(first[...], jnp.concatenate([field, field], 0))
        turned = []
        for f in range(3):
            re = half[:parts, f * rows : (f + 1) * rows]
            im = half[parts:, f * rows : (f + 1) * rows]
            turned.append(jnp.concatenate([re * cos - im * sin, re * sin + im * cos], 1))
        spec = wide(jnp.concatenate(turned, 0), second)
        (xr, xi), (kr, ki), (gr, gi) = [
            (spec[f * parts : (f + 1) * parts, :rows], spec[f * parts : (f + 1) * parts, rows:])
            for f in range(3)
        ]
        long_spec = jnp.concatenate([xr * kr - xi * ki, xr * ki + xi * kr], 1)
        mixed_spec = jnp.concatenate([kr * gr + ki * gi, kr * gi - ki * gr], 1)
        filter_spec = jnp.concatenate([xr * gr + xi * gi, xr * gi - xi * gr], 1)
        part = wide(jnp.concatenate([long_spec, mixed_spec, filter_spec], 0), back)
        turned = []
        for f in range(3):
            re = part[f * parts : (f + 1) * parts, :rows]
            im = part[f * parts : (f + 1) * parts, rows:]
            turned.append(jnp.concatenate([re * cos + im * sin, im * cos - re * sin], 0))
        high, low = split(jnp.concatenate(turned, 1))
        result = dot(last[...], jnp.concatenate([high, low, high], 0))
        for f in range(3):
            buf[places[f], :] = result[:, f * rows : (f + 1) * rows]
    out[...] = buf[...].reshape(parts, lines, rows).astype(bf16)


def gate_kernel(landed, qs, ks, vs, gg, wo, gq, gk, gv, heads, gated, other):
    rows, width = qs.shape
    parts, lines, _ = landed.shape
    group = lines // 3
    for first in range(0, width, WIDE):
        part = slice(first, first + WIDE)
        values = landed[first // group : (first + WIDE) // group].astype(f32)
        long_out, grad_mixed = [
            values[:, f * group : (f + 1) * group, :].reshape(WIDE, rows).T for f in range(2)
        ]
        gated[:, part] = (qs[:, part] * long_out).astype(bf16)
        for which, (to, value) in enumerate(
            (
                (gq, gg[:, part] * long_out),
                (gk, grad_mixed * vs[:, part]),
                (gv, grad_mixed * ks[:, part]),
            )
        ):
            to[:, part] = value
            heads[which, :, part] = value[:TAIL, :].astype(bf16)
    for first in range(0, width, WIDE):
        part = slice(first, first + WIDE)
        other[:, part] = jnp.dot(gated[...], wo[:, part], preferred_element_type=f32)


def project_kernel(landed, gated, wm, gf, mine):
    rows, width = gated.shape
    parts, lines, _ = landed.shape
    group = lines // 3
    for first in range(0, width, WIDE):
        part = slice(first, first + WIDE)
        mine[:, part] = jnp.dot(gated[...], wm[:, part], preferred_element_type=f32)
        values = landed[first // group : (first + WIDE) // group].astype(f32)
        gf[:, part] = values[:, 2 * group :, :].reshape(WIDE, rows).T


def close_kernel(gq, gk, gv, after, taps, mine, other, block_out, oq, ok, ov, pad):
    rows, width = gq.shape
    for which, (value, to) in enumerate(((gq, oq), (gk, ok), (gv, ov))):
        pad[0:rows, :] = value[...]
        pad[rows : rows + EDGE, :] = after[which].astype(f32)[:EDGE, :]
        total = taps[which, 0:1, :] * pad[0:rows, :]
        for shift in range(1, taps.shape[1]):
            total = total + taps[which, shift : shift + 1, :] * pad[shift : shift + rows, :]
        to[...] = total.astype(bf16)
    block_out[...] = (mine[...] + other[...]).astype(bf16)


def on_device(query_in, key_in, value_in, taps, long_filter, out_weight, out_grad):
    rows, width = query_in.shape
    parts = lax.axis_size("ctx")
    seq_total = parts * rows
    group = width // parts
    lines = 3 * group
    reach = taps.shape[1]
    outs = out_weight.shape[1]
    here = lax.axis_index("ch").astype(jnp.int32).reshape(1)
    gain = 1.0 / math.sqrt(seq_total) / seq_total
    swap = [(0, 1), (1, 0)]
    order = ring_order(parts)

    params = pltpu.CompilerParams(vmem_limit_bytes=VMEM_LIMIT)
    vmem = pl.BlockSpec(memory_space=pltpu.VMEM)
    hbm = pl.BlockSpec(memory_space=pltpu.HBM)
    smem = pl.BlockSpec(memory_space=pltpu.SMEM)
    flat = jax.ShapeDtypeStruct((rows, width), f32)
    half = jax.ShapeDtypeStruct((rows, width), bf16)
    fields = jax.ShapeDtypeStruct((parts, lines, rows), bf16)
    edges = jax.ShapeDtypeStruct((3, TAIL, width), bf16)
    weights = jax.ShapeDtypeStruct((width, outs // 2), bf16)
    cost = pl.CostEstimate(flops=2 * rows * width * outs, bytes_accessed=8 * 2**20, transcendentals=0)

    grad_other = lax.ppermute(out_grad, "ch", swap)
    far = [
        pltpu.with_memory_space_constraint(x, pltpu.HBM)
        for x in (query_in, key_in, value_in, long_filter, out_grad, out_weight, taps)
    ]
    with jax.named_scope("tails"):
        tails = pl.pallas_call(
            tails_kernel,
            in_specs=[hbm] * 3,
            out_specs=vmem,
            out_shape=edges,
            scratch_shapes=[pltpu.SemaphoreType.DMA((3,))],
            compiler_params=params,
        )(*far[:3])
    halo = shifted(tails, "ctx", 1)

    with jax.named_scope("fetch"):
        qs, ks, vs, gg, ft, wm, wo, taps_near = pl.pallas_call(
            fetch_kernel,
            in_specs=[smem] + [hbm] * 7,
            out_specs=[vmem] * 8,
            out_shape=[
                flat,
                flat,
                flat,
                flat,
                jax.ShapeDtypeStruct((width, rows), f32),
                weights,
                weights,
                jax.ShapeDtypeStruct(taps.shape, f32),
            ],
            scratch_shapes=[
                pltpu.VMEM((rows, width), bf16),
                pltpu.VMEM((rows, width), bf16),
                pltpu.VMEM((rows, width), bf16),
                pltpu.VMEM((rows, width), f32),
                pltpu.VMEM((rows, width), bf16),
                pltpu.VMEM((rows + EDGE, WIDE), f32),
                pltpu.SemaphoreType.DMA((8,)),
            ],
            compiler_params=params,
            cost_estimate=cost,
        )(here, *far)

    with jax.named_scope("prepare"):
        send, qs, ks, vs, gg = pl.pallas_call(
            prepare_kernel,
            in_specs=[vmem] * 9,
            out_specs=[vmem] * 5,
            out_shape=[fields, flat, flat, flat, flat],
            scratch_shapes=[pltpu.VMEM((2 * EDGE, WIDE), f32)],
            compiler_params=params,
        )(halo, taps_near, qs, ks, vs, gg, ft, grad_other, wo)

    arrived = lax.all_to_all(
        send, "ctx", split_axis=0, concat_axis=0, tiled=True, axis_index_groups=[order]
    )

    with jax.named_scope("spectral"):
        solved = pl.pallas_call(
            spectral_kernel,
            out_shape=fields,
            scratch_shapes=[pltpu.VMEM((parts * lines, rows), f32)],
            compiler_params=params,
        )(arrived, *tables(parts, rows, gain, order))

    landed = lax.all_to_all(
        solved, "ctx", split_axis=0, concat_axis=0, tiled=True, axis_index_groups=[order]
    )

    with jax.named_scope("gate"):
        gq, gk, gv, heads, gated, other = pl.pallas_call(
            gate_kernel,
            in_specs=[vmem] * 6,
            out_specs=[vmem] * 6,
            out_shape=[flat, flat, flat, edges, half, flat],
            compiler_params=params,
        )(landed, qs, ks, vs, gg, wo)

    after = shifted(heads, "ctx", -1)
    theirs = lax.ppermute(other, "ch", swap)

    with jax.named_scope("project"):
        grad_filter, mine = pl.pallas_call(
            project_kernel,
            in_specs=[vmem] * 3,
            out_specs=[vmem] * 2,
            out_shape=[flat, flat],
            compiler_params=params,
            cost_estimate=cost,
        )(landed, gated, wm)

    with jax.named_scope("close"):
        column = pl.BlockSpec((rows, WIDE), lambda i: (0, i))
        edge = pl.BlockSpec((3, TAIL, WIDE), lambda i: (0, 0, i))
        taps_spec = pl.BlockSpec((3, reach, WIDE), lambda i: (0, 0, i))
        block_out, grad_query, grad_key, grad_value = pl.pallas_call(
            close_kernel,
            grid=(width // WIDE,),
            in_specs=[column] * 3 + [edge, taps_spec, column, column],
            out_specs=[column] * 4,
            out_shape=[half] * 4,
            scratch_shapes=[pltpu.VMEM((rows + EDGE, WIDE), f32)],
            compiler_params=params,
        )(gq, gk, gv, after, taps_near, mine, theirs)
    return (block_out, grad_query, grad_key, grad_value, grad_filter)


def solution(mesh):
    return jax.shard_map(
        on_device,
        mesh=mesh,
        in_specs=(
            P("ctx", "ch"),
            P("ctx", "ch"),
            P("ctx", "ch"),
            P(None, None, "ch"),
            P("ctx", "ch"),
            P("ch", None),
            P("ctx", "ch"),
        ),
        out_specs=(P("ctx", "ch"), P("ctx", "ch"), P("ctx", "ch"), P("ctx", "ch"), P("ctx", "ch")),
        check_vma=False,
    )
```

```python
import math

import jax
import jax.numpy as jnp
import ml_dtypes
import numpy as np
from jax import lax
from jax.experimental import pallas as pl
from jax.experimental.pallas import tpu as pltpu
from jax.sharding import PartitionSpec as P

f32 = jnp.float32
bf16 = jnp.bfloat16
EDGE = 8
TAIL = 16
WIDE = 256
VMEM_LIMIT = 24 * 1024 * 1024


def shifted(value, axis, steps):
    count = lax.axis_size(axis)
    first, last = (max(0, -steps), min(count, count - steps))
    return lax.ppermute(value, axis, [(source, source + steps) for source in range(first, last)])


def halves(table):
    high = table.astype(ml_dtypes.bfloat16)
    low = (table - high.astype(np.float64)).astype(ml_dtypes.bfloat16)
    return high, low


def ring_order(parts):
    length = math.gcd(parts, 8)
    ring = [place for place in (0, 4, 2, 6, 1, 5, 3, 7) if place < length]
    plane = parts // length
    return [place * plane + spot for spot in range(plane) for place in ring]


def tables(parts, rows, gain, order):
    freqs = np.arange(parts) + 0.5
    blocks = np.asarray(order)
    inner = np.arange(rows)
    outer = np.outer(freqs, blocks) * (-2.0 * math.pi / (2 * parts))
    turn = np.outer(freqs, inner) * (-2.0 * math.pi / (2 * parts * rows))
    small = np.outer(inner, inner) % rows * (-2.0 * math.pi / rows)
    first = halves(np.concatenate([np.cos(outer), np.sin(outer)], 0))
    first = np.concatenate(first, 1)
    c, s = np.cos(small), np.sin(small)
    high, low = halves(np.block([[c, s], [-s, c]]))
    second = np.stack([high, low])
    high, low = halves(np.block([[c, -s], [s, c]]))
    back = np.stack([high, low])
    high, low = halves(np.concatenate([np.cos(outer).T, np.sin(outer).T], 1) * gain)
    last = np.concatenate([high, low], 0)
    twist = np.stack([np.cos(turn), np.sin(turn)]).astype(np.float32)
    return first, second, back, last, twist


def split(value):
    high = value.astype(bf16)
    low = (value - high.astype(f32)).astype(bf16)
    return high, low


def tails_kernel(q, k, v, out, sems):
    rows = q.shape[0]
    copies = [
        pltpu.make_async_copy(x.at[pl.ds(rows - TAIL, TAIL), :], out.at[which], sems.at[which])
        for which, x in enumerate((q, k, v))
    ]
    for copy in copies:
        copy.start()
    for copy in copies:
        copy.wait()


ACROSS = (((1,), (1,)), ((), ()))


def fetch_kernel(
    here, q, k, v, filt, mine, w, taps_in, qs, ks, vs, gg, ft, wm, wo, taps, qb, kb, vb, fb, mb, pad, sems
):
    rows, width = q.shape
    half = w.shape[1] // 2
    me = here[0]
    w_mine = w.at[:, pl.ds(pl.multiple_of(me * half, half), half)]
    w_other = w.at[:, pl.ds(pl.multiple_of((1 - me) * half, half), half)]
    pairs = ((taps_in, taps), (q, qb), (k, kb), (v, vb), (filt, fb), (mine, mb), (w_mine, wm), (w_other, wo))
    copies = [pltpu.make_async_copy(src, dst, sems.at[i]) for i, (src, dst) in enumerate(pairs)]
    for copy in copies:
        copy.start()
    pad[0:EDGE, :] = jnp.zeros((EDGE, WIDE), f32)
    copies[0].wait()
    for which, (buf, out) in enumerate(((qb, qs), (kb, ks), (vb, vs))):
        copies[1 + which].wait()
        for first in range(0, width, WIDE):
            columns = slice(first, first + WIDE)
            pad[EDGE : EDGE + rows, :] = buf[:, columns].astype(f32)
            total = taps[which, 0:1, columns] * pad[EDGE : EDGE + rows, :]
            for shift in range(1, taps.shape[1]):
                moved = pad[EDGE - shift : EDGE - shift + rows, :]
                total = total + taps[which, shift : shift + 1, columns] * moved
            out[:, columns] = total
    copies[4].wait()
    for first in range(0, width, WIDE):
        ft[first : first + WIDE, :] = fb[:, first : first + WIDE].T
    copies[5].wait()
    copies[6].wait()
    for first in range(0, width, WIDE):
        part = slice(first, first + WIDE)
        gg[:, part] = lax.dot_general(mb[...], wm[part, :], ACROSS, preferred_element_type=f32)
    copies[7].wait()


def prepare_kernel(halo, taps, qs_in, ks_in, vs_in, gg_in, ft, other, wo, send, qs, ks, vs, gg, pad):
    rows, width = gg.shape
    parts, lines, _ = send.shape
    group = lines // 3
    pad[EDGE : 2 * EDGE, :] = jnp.zeros((EDGE, WIDE), f32)
    for first in range(0, width, WIDE):
        part = slice(first, first + WIDE)
        grad = gg_in[:, part] + lax.dot_general(other[...], wo[part, :], ACROSS, preferred_element_type=f32)
        gg[:, part] = grad
        shorts = []
        for which, (before, after) in enumerate(((qs_in, qs), (ks_in, ks), (vs_in, vs))):
            pad[0:EDGE, :] = halo[which, :, part].astype(f32)[TAIL - EDGE :, :]
            top = before[0:EDGE, part]
            for shift in range(1, taps.shape[1]):
                top = top + taps[which, shift : shift + 1, part] * pad[EDGE - shift : 2 * EDGE - shift, :]
            value = jnp.concatenate([top, before[EDGE:, part]], 0)
            after[:, part] = value
            shorts.append(value)
        mixed = (shorts[1] * shorts[2]).T
        grad_long = (grad * shorts[0]).T
        turned = [field.reshape(WIDE // group, group, rows) for field in (mixed, ft[part, :], grad_long)]
        send[first // group : (first + WIDE) // group] = jnp.concatenate(turned, axis=1).astype(bf16)


BATCH = 4


def spectral_kernel(x, first, second, back, last, twist, out, buf):
    parts, lines, rows = x.shape
    group = lines // 3
    buf[...] = x[...].astype(f32).reshape(parts * lines, rows)
    cos, sin = twist[0], twist[1]

    def dot(left, right):
        return jnp.dot(left, right, preferred_element_type=f32)

    def wide(value, table):
        high, low = split(value)
        count = value.shape[0]
        both = dot(jnp.concatenate([high, low], 0), table[0])
        return both[:count] + both[count:] + dot(high, table[1])

    def spot(f, c):
        return pl.ds(f * group + c, parts, stride=lines)

    for base in range(0, group, BATCH):
        lanes = range(base, min(base + BATCH, group))
        turned = []
        for c in lanes:
            field = jnp.concatenate([buf[spot(f, c), :] for f in range(3)], 1).astype(bf16)
            half = dot(first[...], jnp.concatenate([field, field], 0))
            for f in range(3):
                re = half[:parts, f * rows : (f + 1) * rows]
                im = half[parts:, f * rows : (f + 1) * rows]
                turned.append(jnp.concatenate([re * cos - im * sin, re * sin + im * cos], 1))
        spec = wide(jnp.concatenate(turned, 0), second)
        solved = []
        for i in range(len(lanes)):
            (xr, xi), (kr, ki), (gr, gi) = [
                (spec[f * parts : (f + 1) * parts, :rows], spec[f * parts : (f + 1) * parts, rows:])
                for f in range(3 * i, 3 * i + 3)
            ]
            solved.append(jnp.concatenate([xr * kr - xi * ki, xr * ki + xi * kr], 1))
            solved.append(jnp.concatenate([kr * gr + ki * gi, kr * gi - ki * gr], 1))
            solved.append(jnp.concatenate([xr * gr + xi * gi, xr * gi - xi * gr], 1))
        part = wide(jnp.concatenate(solved, 0), back)
        turned = []
        for f in range(3 * len(lanes)):
            re = part[f * parts : (f + 1) * parts, :rows]
            im = part[f * parts : (f + 1) * parts, rows:]
            turned.append(jnp.concatenate([re * cos + im * sin, im * cos - re * sin], 0))
        high, low = split(jnp.concatenate(turned, 1))
        both = dot(last[...], high)
        result = both[:parts] + both[parts:] + dot(last[:parts, :], low)
        for i, c in enumerate(lanes):
            for f in range(3):
                place = (3 * i + f) * rows
                buf[spot(f, c), :] = result[:, place : place + rows]
    out[...] = buf[...].reshape(parts, lines, rows).astype(bf16)


def gate_kernel(landed, qs, ks, vs, gg, wo, gq, gk, gv, heads, gated, other):
    rows, width = qs.shape
    parts, lines, _ = landed.shape
    group = lines // 3
    for first in range(0, width, WIDE):
        part = slice(first, first + WIDE)
        values = landed[first // group : (first + WIDE) // group].astype(f32)
        long_out, grad_mixed = [
            values[:, f * group : (f + 1) * group, :].reshape(WIDE, rows).T for f in range(2)
        ]
        gated[:, part] = (qs[:, part] * long_out).astype(bf16)
        for which, (to, value) in enumerate(
            (
                (gq, gg[:, part] * long_out),
                (gk, grad_mixed * vs[:, part]),
                (gv, grad_mixed * ks[:, part]),
            )
        ):
            to[:, part] = value
            heads[which, :, part] = value[:TAIL, :].astype(bf16)
    for first in range(0, width, WIDE):
        part = slice(first, first + WIDE)
        other[:, part] = jnp.dot(gated[...], wo[:, part], preferred_element_type=f32)


def project_kernel(landed, gated, wm, gq, gk, gv, taps, gf, mine, tq, tk, tv, pad):
    rows, width = gated.shape
    parts, lines, _ = landed.shape
    group = lines // 3
    pad[rows : rows + EDGE, :] = jnp.zeros((EDGE, WIDE), f32)
    for first in range(0, width, WIDE):
        part = slice(first, first + WIDE)
        mine[:, part] = jnp.dot(gated[...], wm[:, part], preferred_element_type=f32)
        values = landed[first // group : (first + WIDE) // group].astype(f32)
        gf[:, part] = values[:, 2 * group :, :].reshape(WIDE, rows).T
        for which, (value, to) in enumerate(((gq, tq), (gk, tk), (gv, tv))):
            pad[0:rows, :] = value[:, part]
            total = taps[which, 0:1, part] * value[:, part]
            for shift in range(1, taps.shape[1]):
                total = total + taps[which, shift : shift + 1, part] * pad[shift : shift + rows, :]
            to[:, part] = total


def close_kernel(tq, tk, tv, after, taps, mine, other, block_out, oq, ok, ov, pad):
    rows, width = tq.shape
    pad[0:EDGE, :] = jnp.zeros((EDGE, width), f32)
    for which, (value, to) in enumerate(((tq, oq), (tk, ok), (tv, ov))):
        pad[EDGE : 2 * EDGE, :] = after[which].astype(f32)[:EDGE, :]
        end = value[rows - EDGE :, :]
        for shift in range(1, taps.shape[1]):
            end = end + taps[which, shift : shift + 1, :] * pad[shift : shift + EDGE, :]
        to[...] = jnp.concatenate([value[: rows - EDGE, :], end], 0).astype(bf16)
    block_out[...] = (mine[...] + other[...]).astype(bf16)


def on_device(query_in, key_in, value_in, taps, long_filter, out_weight, out_grad):
    rows, width = query_in.shape
    parts = lax.axis_size("ctx")
    seq_total = parts * rows
    group = width // parts
    lines = 3 * group
    reach = taps.shape[1]
    outs = out_weight.shape[1]
    here = lax.axis_index("ch").astype(jnp.int32).reshape(1)
    gain = 1.0 / math.sqrt(seq_total) / seq_total
    swap = [(0, 1), (1, 0)]
    order = ring_order(parts)

    params = pltpu.CompilerParams(vmem_limit_bytes=VMEM_LIMIT)
    vmem = pl.BlockSpec(memory_space=pltpu.VMEM)
    hbm = pl.BlockSpec(memory_space=pltpu.HBM)
    smem = pl.BlockSpec(memory_space=pltpu.SMEM)
    flat = jax.ShapeDtypeStruct((rows, width), f32)
    half = jax.ShapeDtypeStruct((rows, width), bf16)
    fields = jax.ShapeDtypeStruct((parts, lines, rows), bf16)
    edges = jax.ShapeDtypeStruct((3, TAIL, width), bf16)
    weights = jax.ShapeDtypeStruct((width, outs // 2), bf16)
    cost = pl.CostEstimate(flops=2 * rows * width * outs, bytes_accessed=8 * 2**20, transcendentals=0)

    grad_other = lax.ppermute(out_grad, "ch", swap)
    far = [
        pltpu.with_memory_space_constraint(x, pltpu.HBM)
        for x in (query_in, key_in, value_in, long_filter, out_grad, out_weight, taps)
    ]
    with jax.named_scope("tails"):
        tails = pl.pallas_call(
            tails_kernel,
            in_specs=[hbm] * 3,
            out_specs=vmem,
            out_shape=edges,
            scratch_shapes=[pltpu.SemaphoreType.DMA((3,))],
            compiler_params=params,
        )(*far[:3])
    halo = shifted(tails, "ctx", 1)

    with jax.named_scope("fetch"):
        qs, ks, vs, gg, ft, wm, wo, taps_near = pl.pallas_call(
            fetch_kernel,
            in_specs=[smem] + [hbm] * 7,
            out_specs=[vmem] * 8,
            out_shape=[
                flat,
                flat,
                flat,
                flat,
                jax.ShapeDtypeStruct((width, rows), f32),
                weights,
                weights,
                jax.ShapeDtypeStruct(taps.shape, f32),
            ],
            scratch_shapes=[
                pltpu.VMEM((rows, width), bf16),
                pltpu.VMEM((rows, width), bf16),
                pltpu.VMEM((rows, width), bf16),
                pltpu.VMEM((rows, width), f32),
                pltpu.VMEM((rows, width), bf16),
                pltpu.VMEM((rows + EDGE, WIDE), f32),
                pltpu.SemaphoreType.DMA((8,)),
            ],
            compiler_params=params,
            cost_estimate=cost,
        )(here, *far)

    with jax.named_scope("prepare"):
        send, qs, ks, vs, gg = pl.pallas_call(
            prepare_kernel,
            in_specs=[vmem] * 9,
            out_specs=[vmem] * 5,
            out_shape=[fields, flat, flat, flat, flat],
            scratch_shapes=[pltpu.VMEM((2 * EDGE, WIDE), f32)],
            compiler_params=params,
        )(halo, taps_near, qs, ks, vs, gg, ft, grad_other, wo)

    arrived = lax.all_to_all(
        send, "ctx", split_axis=0, concat_axis=0, tiled=True, axis_index_groups=[order]
    )

    with jax.named_scope("spectral"):
        solved = pl.pallas_call(
            spectral_kernel,
            out_shape=fields,
            scratch_shapes=[pltpu.VMEM((parts * lines, rows), f32)],
            compiler_params=params,
        )(arrived, *tables(parts, rows, gain, order))

    landed = lax.all_to_all(
        solved, "ctx", split_axis=0, concat_axis=0, tiled=True, axis_index_groups=[order]
    )

    with jax.named_scope("gate"):
        gq, gk, gv, heads, gated, other = pl.pallas_call(
            gate_kernel,
            in_specs=[vmem] * 6,
            out_specs=[vmem] * 6,
            out_shape=[flat, flat, flat, edges, half, flat],
            compiler_params=params,
        )(landed, qs, ks, vs, gg, wo)

    after = shifted(heads, "ctx", -1)
    theirs = lax.ppermute(other, "ch", swap)

    with jax.named_scope("project"):
        grad_filter, mine, tq, tk, tv = pl.pallas_call(
            project_kernel,
            in_specs=[vmem] * 7,
            out_specs=[vmem] * 5,
            out_shape=[flat] * 5,
            scratch_shapes=[pltpu.VMEM((rows + EDGE, WIDE), f32)],
            compiler_params=params,
            cost_estimate=cost,
        )(landed, gated, wm, gq, gk, gv, taps_near)

    with jax.named_scope("close"):
        column = pl.BlockSpec((rows, WIDE), lambda i: (0, i))
        edge = pl.BlockSpec((3, TAIL, WIDE), lambda i: (0, 0, i))
        taps_spec = pl.BlockSpec((3, reach, WIDE), lambda i: (0, 0, i))
        block_out, grad_query, grad_key, grad_value = pl.pallas_call(
            close_kernel,
            grid=(width // WIDE,),
            in_specs=[column] * 3 + [edge, taps_spec, column, column],
            out_specs=[column] * 4,
            out_shape=[half] * 4,
            scratch_shapes=[pltpu.VMEM((2 * EDGE, WIDE), f32)],
            compiler_params=params,
        )(tq, tk, tv, after, taps_near, mine, theirs)
    return (block_out, grad_query, grad_key, grad_value, grad_filter)


def solution(mesh):
    return jax.shard_map(
        on_device,
        mesh=mesh,
        in_specs=(
            P("ctx", "ch"),
            P("ctx", "ch"),
            P("ctx", "ch"),
            P(None, None, "ch"),
            P("ctx", "ch"),
            P("ch", None),
            P("ctx", "ch"),
        ),
        out_specs=(P("ctx", "ch"), P("ctx", "ch"), P("ctx", "ch"), P("ctx", "ch"), P("ctx", "ch")),
        check_vma=False,
    )
```

```python
import math

import jax
import jax.numpy as jnp
import ml_dtypes
import numpy as np
from jax import lax
from jax.experimental import pallas as pl
from jax.experimental.pallas import tpu as pltpu
from jax.sharding import PartitionSpec as P

f32 = jnp.float32
bf16 = jnp.bfloat16
EDGE = 8
TAIL = 16
WIDE = 256
LANES = 128
VMEM_LIMIT = 24 * 1024 * 1024


def shifted(value, axis, steps):
    count = lax.axis_size(axis)
    first, last = (max(0, -steps), min(count, count - steps))
    return lax.ppermute(value, axis, [(source, source + steps) for source in range(first, last)])


def halves(table):
    high = table.astype(ml_dtypes.bfloat16)
    low = (table - high.astype(np.float64)).astype(ml_dtypes.bfloat16)
    return high, low


def ring_order(parts):
    length = math.gcd(parts, 8)
    ring = [place for place in (0, 4, 2, 6, 1, 5, 3, 7) if place < length]
    plane = parts // length
    return [place * plane + spot for spot in range(plane) for place in ring]


def tables(parts, rows, gain, order):
    freqs = np.arange(parts) + 0.5
    blocks = np.asarray(order)
    inner = np.arange(rows)
    outer = np.outer(freqs, blocks) * (-2.0 * math.pi / (2 * parts))
    turn = np.outer(freqs, inner) * (-2.0 * math.pi / (2 * parts * rows))
    small = np.outer(inner, inner) % rows * (-2.0 * math.pi / rows)
    first = halves(np.concatenate([np.cos(outer), np.sin(outer)], 0))
    first = np.concatenate(first, 1)
    c, s = np.cos(small), np.sin(small)
    high, low = halves(np.block([[c, s], [-s, c]]))
    second = np.stack([high, low])
    high, low = halves(np.block([[c, -s], [s, c]]))
    back = np.stack([high, low])
    high, low = halves(np.concatenate([np.cos(outer).T, np.sin(outer).T], 1) * gain)
    last = np.concatenate([high, low], 0)
    twist = np.stack([np.cos(turn), np.sin(turn)]).astype(np.float32)
    return first, second, back, last, twist


def split(value):
    high = value.astype(bf16)
    low = (value - high.astype(f32)).astype(bf16)
    return high, low


def tails_kernel(q, k, v, out, sems):
    rows = q.shape[0]
    copies = [
        pltpu.make_async_copy(x.at[pl.ds(rows - TAIL, TAIL), :], out.at[which], sems.at[which])
        for which, x in enumerate((q, k, v))
    ]
    for copy in copies:
        copy.start()
    for copy in copies:
        copy.wait()


ACROSS = (((1,), (1,)), ((), ()))


def fetch_kernel(
    here, q, k, v, filt, mine, w, taps_in, qs, ks, vs, gg, ft, wm, wo, taps, qb, kb, vb, fb, mb, pad, sems
):
    rows, width = q.shape
    half = w.shape[1] // 2
    me = here[0]
    w_mine = w.at[:, pl.ds(pl.multiple_of(me * half, half), half)]
    w_other = w.at[:, pl.ds(pl.multiple_of((1 - me) * half, half), half)]
    pairs = ((taps_in, taps), (q, qb), (k, kb), (v, vb), (filt, fb), (mine, mb), (w_mine, wm), (w_other, wo))
    copies = [pltpu.make_async_copy(src, dst, sems.at[i]) for i, (src, dst) in enumerate(pairs)]
    for copy in copies:
        copy.start()
    pad[0:EDGE, :] = jnp.zeros((EDGE, LANES), f32)
    copies[0].wait()
    for which, (buf, out) in enumerate(((qb, qs), (kb, ks), (vb, vs))):
        copies[1 + which].wait()
        for first in range(0, width, LANES):
            columns = slice(first, first + LANES)
            pad[EDGE : EDGE + rows, :] = buf[:, columns].astype(f32)
            total = taps[which, 0:1, columns] * pad[EDGE : EDGE + rows, :]
            for shift in range(1, taps.shape[1]):
                moved = pad[EDGE - shift : EDGE - shift + rows, :]
                total = total + taps[which, shift : shift + 1, columns] * moved
            out[:, columns] = total
    copies[4].wait()
    for first in range(0, width, WIDE):
        ft[first : first + WIDE, :] = fb[:, first : first + WIDE].T
    copies[5].wait()
    copies[6].wait()
    for first in range(0, width, WIDE):
        part = slice(first, first + WIDE)
        gg[:, part] = lax.dot_general(mb[...], wm[part, :], ACROSS, preferred_element_type=f32)
    copies[7].wait()


def prepare_kernel(halo, taps, qs_in, ks_in, vs_in, gg_in, ft, other, wo, send, qs, ks, vs, gg, pad):
    rows, width = gg.shape
    parts, lines, _ = send.shape
    group = lines // 3
    pad[EDGE : 2 * EDGE, :] = jnp.zeros((EDGE, WIDE), f32)
    for first in range(0, width, WIDE):
        part = slice(first, first + WIDE)
        grad = gg_in[:, part] + lax.dot_general(other[...], wo[part, :], ACROSS, preferred_element_type=f32)
        gg[:, part] = grad
        shorts = []
        for which, (before, after) in enumerate(((qs_in, qs), (ks_in, ks), (vs_in, vs))):
            pad[0:EDGE, :] = halo[which, :, part].astype(f32)[TAIL - EDGE :, :]
            top = before[0:EDGE, part]
            for shift in range(1, taps.shape[1]):
                top = top + taps[which, shift : shift + 1, part] * pad[EDGE - shift : 2 * EDGE - shift, :]
            value = jnp.concatenate([top, before[EDGE:, part]], 0)
            after[:, part] = value
            shorts.append(value)
        mixed = (shorts[1] * shorts[2]).T
        grad_long = (grad * shorts[0]).T
        turned = [field.reshape(WIDE // group, group, rows) for field in (mixed, ft[part, :], grad_long)]
        send[first // group : (first + WIDE) // group] = jnp.concatenate(turned, axis=1).astype(bf16)


BATCH = 4


def spectral_kernel(x, first, second, back, last, twist, out, buf):
    parts, lines, rows = x.shape
    group = lines // 3
    buf[...] = x[...].astype(f32).reshape(parts * lines, rows)
    cos, sin = twist[0], twist[1]

    def dot(left, right):
        return jnp.dot(left, right, preferred_element_type=f32)

    def wide(value, table):
        high, low = split(value)
        count = value.shape[0]
        both = dot(jnp.concatenate([high, low], 0), table[0])
        return both[:count] + both[count:] + dot(high, table[1])

    def spot(f, c):
        return pl.ds(f * group + c, parts, stride=lines)

    for base in range(0, group, BATCH):
        lanes = range(base, min(base + BATCH, group))
        turned = []
        for c in lanes:
            field = jnp.concatenate([buf[spot(f, c), :] for f in range(3)], 1).astype(bf16)
            half = dot(first[...], jnp.concatenate([field, field], 0))
            for f in range(3):
                re = half[:parts, f * rows : (f + 1) * rows]
                im = half[parts:, f * rows : (f + 1) * rows]
                turned.append(jnp.concatenate([re * cos - im * sin, re * sin + im * cos], 1))
        spec = wide(jnp.concatenate(turned, 0), second)
        solved = []
        for i in range(len(lanes)):
            (xr, xi), (kr, ki), (gr, gi) = [
                (spec[f * parts : (f + 1) * parts, :rows], spec[f * parts : (f + 1) * parts, rows:])
                for f in range(3 * i, 3 * i + 3)
            ]
            solved.append(jnp.concatenate([xr * kr - xi * ki, xr * ki + xi * kr], 1))
            solved.append(jnp.concatenate([kr * gr + ki * gi, kr * gi - ki * gr], 1))
            solved.append(jnp.concatenate([xr * gr + xi * gi, xr * gi - xi * gr], 1))
        part = wide(jnp.concatenate(solved, 0), back)
        turned = []
        for f in range(3 * len(lanes)):
            re = part[f * parts : (f + 1) * parts, :rows]
            im = part[f * parts : (f + 1) * parts, rows:]
            turned.append(jnp.concatenate([re * cos + im * sin, im * cos - re * sin], 0))
        high, low = split(jnp.concatenate(turned, 1))
        both = dot(last[...], high)
        result = both[:parts] + both[parts:] + dot(last[:parts, :], low)
        for i, c in enumerate(lanes):
            for f in range(3):
                place = (3 * i + f) * rows
                buf[spot(f, c), :] = result[:, place : place + rows]
    out[...] = buf[...].reshape(parts, lines, rows).astype(bf16)


def gate_kernel(landed, qs, gg, wo, gq, gated, other):
    rows, width = qs.shape
    parts, lines, _ = landed.shape
    group = lines // 3
    for first in range(0, width, WIDE):
        part = slice(first, first + WIDE)
        values = landed[first // group : (first + WIDE) // group].astype(f32)
        long_out = values[:, :group, :].reshape(WIDE, rows).T
        gated[:, part] = (qs[:, part] * long_out).astype(bf16)
        gq[:, part] = gg[:, part] * long_out
    for first in range(0, width, WIDE):
        part = slice(first, first + WIDE)
        other[:, part] = jnp.dot(gated[...], wo[:, part], preferred_element_type=f32)


def grads_kernel(landed, ks, vs, gq, gk, gv, gf, heads):
    rows, width = ks.shape
    parts, lines, _ = landed.shape
    group = lines // 3
    for first in range(0, width, WIDE):
        part = slice(first, first + WIDE)
        values = landed[first // group : (first + WIDE) // group].astype(f32)
        grad_mixed, grad_filter = [
            values[:, f * group : (f + 1) * group, :].reshape(WIDE, rows).T for f in (1, 2)
        ]
        grad_k = grad_mixed * vs[:, part]
        grad_v = grad_mixed * ks[:, part]
        gk[:, part] = grad_k
        gv[:, part] = grad_v
        gf[:, part] = grad_filter
        heads[0, :, part] = gq[:TAIL, part].astype(bf16)
        heads[1, :, part] = grad_k[:TAIL].astype(bf16)
        heads[2, :, part] = grad_v[:TAIL].astype(bf16)


def project_kernel(gated, wm, gq, gk, gv, taps, mine, ends, oq, ok, ov, pad):
    rows, width = gated.shape
    for first in range(0, width, WIDE):
        part = slice(first, first + WIDE)
        mine[:, part] = jnp.dot(gated[...], wm[:, part], preferred_element_type=f32)
    pad[rows : rows + EDGE, :] = jnp.zeros((EDGE, LANES), f32)
    for which, (value, to) in enumerate(((gq, oq), (gk, ok), (gv, ov))):
        for first in range(0, width, LANES):
            part = slice(first, first + LANES)
            pad[0:rows, :] = value[:, part]
            total = taps[which, 0:1, part] * value[:, part]
            for shift in range(1, taps.shape[1]):
                total = total + taps[which, shift : shift + 1, part] * pad[shift : shift + rows, :]
            to[:, part] = total.astype(bf16)
            ends[which, :, part] = total[rows - TAIL :, :]


def close_kernel(ends, after, taps, mine, other, near_q, near_k, near_v, block_out, oq, ok, ov, pad, tail, sems):
    rows, width = mine.shape
    pad[0:EDGE, :] = jnp.zeros((EDGE, width), f32)
    copies = []
    for which, to in enumerate((oq, ok, ov)):
        pad[EDGE : 2 * EDGE, :] = after[which].astype(f32)[:EDGE, :]
        end = ends[which, TAIL - EDGE :, :]
        for shift in range(1, taps.shape[1]):
            end = end + taps[which, shift : shift + 1, :] * pad[shift : shift + EDGE, :]
        tail[which] = jnp.concatenate([ends[which, : TAIL - EDGE, :], end], 0).astype(bf16)
        copy = pltpu.make_async_copy(tail.at[which], to.at[pl.ds(rows - TAIL, TAIL), :], sems.at[which])
        copy.start()
        copies.append(copy)
    block_out[...] = (mine[...] + other[...]).astype(bf16)
    for copy in copies:
        copy.wait()


def on_device(query_in, key_in, value_in, taps, long_filter, out_weight, out_grad):
    rows, width = query_in.shape
    parts = lax.axis_size("ctx")
    seq_total = parts * rows
    group = width // parts
    lines = 3 * group
    outs = out_weight.shape[1]
    here = lax.axis_index("ch").astype(jnp.int32).reshape(1)
    gain = 1.0 / math.sqrt(seq_total) / seq_total
    swap = [(0, 1), (1, 0)]
    order = ring_order(parts)

    params = pltpu.CompilerParams(vmem_limit_bytes=VMEM_LIMIT)
    vmem = pl.BlockSpec(memory_space=pltpu.VMEM)
    hbm = pl.BlockSpec(memory_space=pltpu.HBM)
    smem = pl.BlockSpec(memory_space=pltpu.SMEM)
    flat = jax.ShapeDtypeStruct((rows, width), f32)
    half = jax.ShapeDtypeStruct((rows, width), bf16)
    fields = jax.ShapeDtypeStruct((parts, lines, rows), bf16)
    edges = jax.ShapeDtypeStruct((3, TAIL, width), bf16)
    weights = jax.ShapeDtypeStruct((width, outs // 2), bf16)
    cost = pl.CostEstimate(flops=2 * rows * width * outs, bytes_accessed=8 * 2**20, transcendentals=0)

    grad_other = lax.ppermute(out_grad, "ch", swap)
    far = [
        pltpu.with_memory_space_constraint(x, pltpu.HBM)
        for x in (query_in, key_in, value_in, long_filter, out_grad, out_weight, taps)
    ]
    with jax.named_scope("tails"):
        tails = pl.pallas_call(
            tails_kernel,
            in_specs=[hbm] * 3,
            out_specs=vmem,
            out_shape=edges,
            scratch_shapes=[pltpu.SemaphoreType.DMA((3,))],
            compiler_params=params,
        )(*far[:3])
    halo = shifted(tails, "ctx", 1)

    with jax.named_scope("fetch"):
        qs, ks, vs, gg, ft, wm, wo, taps_near = pl.pallas_call(
            fetch_kernel,
            in_specs=[smem] + [hbm] * 7,
            out_specs=[vmem] * 8,
            out_shape=[
                flat,
                flat,
                flat,
                flat,
                jax.ShapeDtypeStruct((width, rows), f32),
                weights,
                weights,
                jax.ShapeDtypeStruct(taps.shape, f32),
            ],
            scratch_shapes=[
                pltpu.VMEM((rows, width), bf16),
                pltpu.VMEM((rows, width), bf16),
                pltpu.VMEM((rows, width), bf16),
                pltpu.VMEM((rows, width), f32),
                pltpu.VMEM((rows, width), bf16),
                pltpu.VMEM((rows + EDGE, LANES), f32),
                pltpu.SemaphoreType.DMA((8,)),
            ],
            compiler_params=params,
            cost_estimate=cost,
        )(here, *far)

    with jax.named_scope("prepare"):
        send, qs, ks, vs, gg = pl.pallas_call(
            prepare_kernel,
            in_specs=[vmem] * 9,
            out_specs=[vmem] * 5,
            out_shape=[fields, flat, flat, flat, flat],
            scratch_shapes=[pltpu.VMEM((2 * EDGE, WIDE), f32)],
            compiler_params=params,
        )(halo, taps_near, qs, ks, vs, gg, ft, grad_other, wo)

    arrived = lax.all_to_all(
        send, "ctx", split_axis=0, concat_axis=0, tiled=True, axis_index_groups=[order]
    )

    with jax.named_scope("spectral"):
        solved = pl.pallas_call(
            spectral_kernel,
            out_shape=fields,
            scratch_shapes=[pltpu.VMEM((parts * lines, rows), f32)],
            compiler_params=params,
        )(arrived, *tables(parts, rows, gain, order))

    landed = lax.all_to_all(
        solved, "ctx", split_axis=0, concat_axis=0, tiled=True, axis_index_groups=[order]
    )

    with jax.named_scope("gate"):
        gq, gated, other = pl.pallas_call(
            gate_kernel,
            in_specs=[vmem] * 4,
            out_specs=[vmem] * 3,
            out_shape=[flat, half, flat],
            compiler_params=params,
        )(landed, qs, gg, wo)
    theirs = lax.ppermute(other, "ch", swap)

    with jax.named_scope("grads"):
        gk, gv, grad_filter, heads = pl.pallas_call(
            grads_kernel,
            in_specs=[vmem] * 4,
            out_specs=[vmem] * 4,
            out_shape=[flat, flat, flat, edges],
            compiler_params=params,
        )(landed, ks, vs, gq)
    after = shifted(heads, "ctx", -1)

    with jax.named_scope("project"):
        mine, ends, oq, ok, ov = pl.pallas_call(
            project_kernel,
            in_specs=[vmem] * 6,
            out_specs=[vmem] * 5,
            out_shape=[flat, jax.ShapeDtypeStruct((3, TAIL, width), f32), half, half, half],
            scratch_shapes=[pltpu.VMEM((rows + EDGE, LANES), f32)],
            compiler_params=params,
            cost_estimate=cost,
        )(gated, wm, gq, gk, gv, taps_near)

    with jax.named_scope("close"):
        begun = [pltpu.with_memory_space_constraint(x, pltpu.HBM) for x in (oq, ok, ov)]
        block_out, grad_query, grad_key, grad_value = pl.pallas_call(
            close_kernel,
            in_specs=[vmem] * 5 + [hbm] * 3,
            out_specs=[vmem] + [hbm] * 3,
            out_shape=[half] * 4,
            input_output_aliases={5: 1, 6: 2, 7: 3},
            scratch_shapes=[
                pltpu.VMEM((2 * EDGE, width), f32),
                pltpu.VMEM((3, TAIL, width), bf16),
                pltpu.SemaphoreType.DMA((3,)),
            ],
            compiler_params=params,
        )(ends, after, taps_near, mine, theirs, *begun)
    return (block_out, grad_query, grad_key, grad_value, grad_filter)


def solution(mesh):
    return jax.shard_map(
        on_device,
        mesh=mesh,
        in_specs=(
            P("ctx", "ch"),
            P("ctx", "ch"),
            P("ctx", "ch"),
            P(None, None, "ch"),
            P("ctx", "ch"),
            P("ch", None),
            P("ctx", "ch"),
        ),
        out_specs=(P("ctx", "ch"), P("ctx", "ch"), P("ctx", "ch"), P("ctx", "ch"), P("ctx", "ch")),
        check_vma=False,
    )
```

```python
import math

import jax
import jax.numpy as jnp
import ml_dtypes
import numpy as np
from jax import lax
from jax.experimental import pallas as pl
from jax.experimental.pallas import tpu as pltpu
from jax.sharding import PartitionSpec as P

f32 = jnp.float32
bf16 = jnp.bfloat16
EDGE = 8
TAIL = 16
WIDE = 256
LANES = 128
VMEM_LIMIT = 24 * 1024 * 1024


def shifted(value, axis, steps):
    count = lax.axis_size(axis)
    first, last = (max(0, -steps), min(count, count - steps))
    return lax.ppermute(value, axis, [(source, source + steps) for source in range(first, last)])


def halves(table):
    high = table.astype(ml_dtypes.bfloat16)
    low = (table - high.astype(np.float64)).astype(ml_dtypes.bfloat16)
    return high, low


def ring_order(parts):
    length = math.gcd(parts, 8)
    ring = [place for place in (0, 4, 2, 6, 1, 5, 3, 7) if place < length]
    plane = parts // length
    return [place * plane + spot for spot in range(plane) for place in ring]


def tables(parts, rows, gain, order):
    freqs = np.arange(parts) + 0.5
    blocks = np.asarray(order)
    inner = np.arange(rows)
    outer = np.outer(freqs, blocks) * (-2.0 * math.pi / (2 * parts))
    turn = np.outer(freqs, inner) * (-2.0 * math.pi / (2 * parts * rows))
    small = np.outer(inner, inner) % rows * (-2.0 * math.pi / rows)
    first = halves(np.concatenate([np.cos(outer), np.sin(outer)], 0))
    first = np.concatenate(first, 1)
    c, s = np.cos(small), np.sin(small)
    high, low = halves(np.block([[c, s], [-s, c]]))
    second = np.stack([high, low])
    high, low = halves(np.block([[c, -s], [s, c]]))
    back = np.stack([high, low])
    high, low = halves(np.concatenate([np.cos(outer).T, np.sin(outer).T], 1) * gain)
    last = np.concatenate([high, low], 0)
    twist = np.stack([np.cos(turn), np.sin(turn)]).astype(np.float32)
    return first, second, back, last, twist


def split(value):
    high = value.astype(bf16)
    low = (value - high.astype(f32)).astype(bf16)
    return high, low


def tails_kernel(q, k, v, out, sems):
    rows = q.shape[0]
    copies = [
        pltpu.make_async_copy(x.at[pl.ds(rows - TAIL, TAIL), :], out.at[which], sems.at[which])
        for which, x in enumerate((q, k, v))
    ]
    for copy in copies:
        copy.start()
    for copy in copies:
        copy.wait()


ACROSS = (((1,), (1,)), ((), ()))


def fetch_kernel(
    here, q, k, v, filt, mine, w, taps_in, qs, ks, vs, gg, ft, wm, wo, taps, qb, kb, vb, fb, mb, pad, sems
):
    rows, width = q.shape
    half = w.shape[1] // 2
    me = here[0]
    w_mine = w.at[:, pl.ds(pl.multiple_of(me * half, half), half)]
    w_other = w.at[:, pl.ds(pl.multiple_of((1 - me) * half, half), half)]
    pairs = ((taps_in, taps), (q, qb), (k, kb), (v, vb), (filt, fb), (mine, mb), (w_mine, wm), (w_other, wo))
    copies = [pltpu.make_async_copy(src, dst, sems.at[i]) for i, (src, dst) in enumerate(pairs)]
    for copy in copies:
        copy.start()
    pad[0:EDGE, :] = jnp.zeros((EDGE, LANES), f32)
    copies[0].wait()
    for which, (buf, out) in enumerate(((qb, qs), (kb, ks), (vb, vs))):
        copies[1 + which].wait()
        for first in range(0, width, LANES):
            columns = slice(first, first + LANES)
            pad[EDGE : EDGE + rows, :] = buf[:, columns].astype(f32)
            total = taps[which, 0:1, columns] * pad[EDGE : EDGE + rows, :]
            for shift in range(1, taps.shape[1]):
                moved = pad[EDGE - shift : EDGE - shift + rows, :]
                total = total + taps[which, shift : shift + 1, columns] * moved
            out[:, columns] = total
    copies[4].wait()
    for first in range(0, width, WIDE):
        ft[first : first + WIDE, :] = fb[:, first : first + WIDE].T
    copies[5].wait()
    copies[6].wait()
    for first in range(0, width, WIDE):
        part = slice(first, first + WIDE)
        gg[:, part] = lax.dot_general(mb[...], wm[part, :], ACROSS, preferred_element_type=f32)
    copies[7].wait()


def prepare_kernel(halo, taps, qs_in, ks_in, vs_in, gg_in, ft, other, wo, send, qs, ks, vs, gg, pad):
    rows, width = gg.shape
    parts, lines, _ = send.shape
    group = lines // 3
    pad[EDGE : 2 * EDGE, :] = jnp.zeros((EDGE, WIDE), f32)
    for first in range(0, width, WIDE):
        part = slice(first, first + WIDE)
        grad = gg_in[:, part] + lax.dot_general(other[...], wo[part, :], ACROSS, preferred_element_type=f32)
        gg[:, part] = grad
        shorts = []
        for which, (before, after) in enumerate(((qs_in, qs), (ks_in, ks), (vs_in, vs))):
            pad[0:EDGE, :] = halo[which, :, part].astype(f32)[TAIL - EDGE :, :]
            top = before[0:EDGE, part]
            for shift in range(1, taps.shape[1]):
                top = top + taps[which, shift : shift + 1, part] * pad[EDGE - shift : 2 * EDGE - shift, :]
            value = jnp.concatenate([top, before[EDGE:, part]], 0)
            after[:, part] = value
            shorts.append(value)
        mixed = (shorts[1] * shorts[2]).T
        grad_long = (grad * shorts[0]).T
        turned = [field.reshape(WIDE // group, group, rows) for field in (mixed, ft[part, :], grad_long)]
        send[first // group : (first + WIDE) // group] = jnp.concatenate(turned, axis=1).astype(bf16)


BATCH = 4


def spectral_kernel(x, first, second, back, last, twist, out, buf):
    parts, lines, rows = x.shape
    group = lines // 3
    buf[...] = x[...].astype(f32).reshape(parts * lines, rows)
    cos, sin = twist[0], twist[1]

    def dot(left, right):
        return jnp.dot(left, right, preferred_element_type=f32)

    def wide(value, table):
        high, low = split(value)
        count = value.shape[0]
        both = dot(jnp.concatenate([high, low], 0), table[0])
        return both[:count] + both[count:] + dot(high, table[1])

    def spot(f, c):
        return pl.ds(f * group + c, parts, stride=lines)

    for base in range(0, group, BATCH):
        lanes = range(base, min(base + BATCH, group))
        turned = []
        for c in lanes:
            field = jnp.concatenate([buf[spot(f, c), :] for f in range(3)], 1).astype(bf16)
            half = dot(first[...], jnp.concatenate([field, field], 0))
            for f in range(3):
                re = half[:parts, f * rows : (f + 1) * rows]
                im = half[parts:, f * rows : (f + 1) * rows]
                turned.append(jnp.concatenate([re * cos - im * sin, re * sin + im * cos], 1))
        spec = wide(jnp.concatenate(turned, 0), second)
        solved = []
        for i in range(len(lanes)):
            (xr, xi), (kr, ki), (gr, gi) = [
                (spec[f * parts : (f + 1) * parts, :rows], spec[f * parts : (f + 1) * parts, rows:])
                for f in range(3 * i, 3 * i + 3)
            ]
            solved.append(jnp.concatenate([xr * kr - xi * ki, xr * ki + xi * kr], 1))
            solved.append(jnp.concatenate([kr * gr + ki * gi, kr * gi - ki * gr], 1))
            solved.append(jnp.concatenate([xr * gr + xi * gi, xr * gi - xi * gr], 1))
        part = wide(jnp.concatenate(solved, 0), back)
        turned = []
        for f in range(3 * len(lanes)):
            re = part[f * parts : (f + 1) * parts, :rows]
            im = part[f * parts : (f + 1) * parts, rows:]
            turned.append(jnp.concatenate([re * cos + im * sin, im * cos - re * sin], 0))
        high, low = split(jnp.concatenate(turned, 1))
        both = dot(last[...], high)
        result = both[:parts] + both[parts:] + dot(last[:parts, :], low)
        for i, c in enumerate(lanes):
            for f in range(3):
                place = (3 * i + f) * rows
                buf[spot(f, c), :] = result[:, place : place + rows]
    out[...] = buf[...].reshape(parts, lines, rows).astype(bf16)


def gate_kernel(landed, qs, ks, vs, gg, wo, gq, gk, gv, heads, gated, other):
    rows, width = qs.shape
    parts, lines, _ = landed.shape
    group = lines // 3
    for first in range(0, width, WIDE):
        part = slice(first, first + WIDE)
        values = landed[first // group : (first + WIDE) // group].astype(f32)
        long_out, grad_mixed = [
            values[:, f * group : (f + 1) * group, :].reshape(WIDE, rows).T for f in range(2)
        ]
        gated[:, part] = (qs[:, part] * long_out).astype(bf16)
        for which, (to, value) in enumerate(
            (
                (gq, gg[:, part] * long_out),
                (gk, grad_mixed * vs[:, part]),
                (gv, grad_mixed * ks[:, part]),
            )
        ):
            to[:, part] = value
            heads[which, :, part] = value[:TAIL, :].astype(bf16)
    for first in range(0, width, WIDE):
        part = slice(first, first + WIDE)
        other[:, part] = jnp.dot(gated[...], wo[:, part], preferred_element_type=f32)


def project_kernel(
    landed, gated, wm, gq, gk, gv, taps, gf, mine, ends, oq, ok, ov, pad, turned, rounded, sems
):
    rows, width = gated.shape
    parts, lines, _ = landed.shape
    group = lines // 3
    for first in range(0, width, WIDE):
        part = slice(first, first + WIDE)
        values = landed[first // group : (first + WIDE) // group].astype(f32)
        turned[:, part] = values[:, 2 * group :, :].reshape(WIDE, rows).T
    copies = [pltpu.make_async_copy(turned, gf, sems.at[3])]
    copies[0].start()
    pad[rows : rows + EDGE, :] = jnp.zeros((EDGE, LANES), f32)
    for which, (value, to) in enumerate(((gq, oq), (gk, ok), (gv, ov))):
        for first in range(0, width, LANES):
            part = slice(first, first + LANES)
            pad[0:rows, :] = value[:, part]
            total = taps[which, 0:1, part] * value[:, part]
            for shift in range(1, taps.shape[1]):
                total = total + taps[which, shift : shift + 1, part] * pad[shift : shift + rows, :]
            rounded[which, :, part] = total.astype(bf16)
            ends[which, :, part] = total[rows - TAIL :, :]
        copy = pltpu.make_async_copy(rounded.at[which], to, sems.at[which])
        copy.start()
        copies.append(copy)
    for first in range(0, width, WIDE):
        part = slice(first, first + WIDE)
        mine[:, part] = jnp.dot(gated[...], wm[:, part], preferred_element_type=f32)
    for copy in copies:
        copy.wait()


def close_kernel(
    ends, after, taps, mine, other, near_q, near_k, near_v, block_out, oq, ok, ov, pad, tail, total, sems
):
    rows, width = mine.shape
    total[...] = (mine[...] + other[...]).astype(bf16)
    copies = [pltpu.make_async_copy(total, block_out, sems.at[3])]
    copies[0].start()
    pad[0:EDGE, :] = jnp.zeros((EDGE, width), f32)
    for which, to in enumerate((oq, ok, ov)):
        pad[EDGE : 2 * EDGE, :] = after[which].astype(f32)[:EDGE, :]
        end = ends[which, TAIL - EDGE :, :]
        for shift in range(1, taps.shape[1]):
            end = end + taps[which, shift : shift + 1, :] * pad[shift : shift + EDGE, :]
        tail[which] = jnp.concatenate([ends[which, : TAIL - EDGE, :], end], 0).astype(bf16)
        copy = pltpu.make_async_copy(tail.at[which], to.at[pl.ds(rows - TAIL, TAIL), :], sems.at[which])
        copy.start()
        copies.append(copy)
    for copy in copies:
        copy.wait()


def on_device(query_in, key_in, value_in, taps, long_filter, out_weight, out_grad):
    rows, width = query_in.shape
    parts = lax.axis_size("ctx")
    seq_total = parts * rows
    group = width // parts
    lines = 3 * group
    outs = out_weight.shape[1]
    here = lax.axis_index("ch").astype(jnp.int32).reshape(1)
    gain = 1.0 / math.sqrt(seq_total) / seq_total
    swap = [(0, 1), (1, 0)]
    order = ring_order(parts)

    params = pltpu.CompilerParams(vmem_limit_bytes=VMEM_LIMIT)
    vmem = pl.BlockSpec(memory_space=pltpu.VMEM)
    hbm = pl.BlockSpec(memory_space=pltpu.HBM)
    smem = pl.BlockSpec(memory_space=pltpu.SMEM)
    flat = jax.ShapeDtypeStruct((rows, width), f32)
    half = jax.ShapeDtypeStruct((rows, width), bf16)
    fields = jax.ShapeDtypeStruct((parts, lines, rows), bf16)
    edges = jax.ShapeDtypeStruct((3, TAIL, width), bf16)
    weights = jax.ShapeDtypeStruct((width, outs // 2), bf16)
    cost = pl.CostEstimate(flops=2 * rows * width * outs, bytes_accessed=8 * 2**20, transcendentals=0)

    grad_other = lax.ppermute(out_grad, "ch", swap)
    far = [
        pltpu.with_memory_space_constraint(x, pltpu.HBM)
        for x in (query_in, key_in, value_in, long_filter, out_grad, out_weight, taps)
    ]
    with jax.named_scope("tails"):
        tails = pl.pallas_call(
            tails_kernel,
            in_specs=[hbm] * 3,
            out_specs=vmem,
            out_shape=edges,
            scratch_shapes=[pltpu.SemaphoreType.DMA((3,))],
            compiler_params=params,
        )(*far[:3])
    halo = shifted(tails, "ctx", 1)

    with jax.named_scope("fetch"):
        qs, ks, vs, gg, ft, wm, wo, taps_near = pl.pallas_call(
            fetch_kernel,
            in_specs=[smem] + [hbm] * 7,
            out_specs=[vmem] * 8,
            out_shape=[
                flat,
                flat,
                flat,
                flat,
                jax.ShapeDtypeStruct((width, rows), f32),
                weights,
                weights,
                jax.ShapeDtypeStruct(taps.shape, f32),
            ],
            scratch_shapes=[
                pltpu.VMEM((rows, width), bf16),
                pltpu.VMEM((rows, width), bf16),
                pltpu.VMEM((rows, width), bf16),
                pltpu.VMEM((rows, width), f32),
                pltpu.VMEM((rows, width), bf16),
                pltpu.VMEM((rows + EDGE, LANES), f32),
                pltpu.SemaphoreType.DMA((8,)),
            ],
            compiler_params=params,
            cost_estimate=cost,
        )(here, *far)

    with jax.named_scope("prepare"):
        send, qs, ks, vs, gg = pl.pallas_call(
            prepare_kernel,
            in_specs=[vmem] * 9,
            out_specs=[vmem] * 5,
            out_shape=[fields, flat, flat, flat, flat],
            scratch_shapes=[pltpu.VMEM((2 * EDGE, WIDE), f32)],
            compiler_params=params,
        )(halo, taps_near, qs, ks, vs, gg, ft, grad_other, wo)

    arrived = lax.all_to_all(
        send, "ctx", split_axis=0, concat_axis=0, tiled=True, axis_index_groups=[order]
    )

    with jax.named_scope("spectral"):
        solved = pl.pallas_call(
            spectral_kernel,
            out_shape=fields,
            scratch_shapes=[pltpu.VMEM((parts * lines, rows), f32)],
            compiler_params=params,
        )(arrived, *tables(parts, rows, gain, order))

    landed = lax.all_to_all(
        solved, "ctx", split_axis=0, concat_axis=0, tiled=True, axis_index_groups=[order]
    )

    with jax.named_scope("gate"):
        gq, gk, gv, heads, gated, other = pl.pallas_call(
            gate_kernel,
            in_specs=[vmem] * 6,
            out_specs=[vmem] * 6,
            out_shape=[flat, flat, flat, edges, half, flat],
            compiler_params=params,
        )(landed, qs, ks, vs, gg, wo)

    after = shifted(heads, "ctx", -1)
    theirs = lax.ppermute(other, "ch", swap)

    with jax.named_scope("project"):
        grad_filter, mine, ends, oq, ok, ov = pl.pallas_call(
            project_kernel,
            in_specs=[vmem] * 7,
            out_specs=[hbm, vmem, vmem, hbm, hbm, hbm],
            out_shape=[flat, flat, jax.ShapeDtypeStruct((3, TAIL, width), f32), half, half, half],
            scratch_shapes=[
                pltpu.VMEM((rows + EDGE, LANES), f32),
                pltpu.VMEM((rows, width), f32),
                pltpu.VMEM((3, rows, width), bf16),
                pltpu.SemaphoreType.DMA((4,)),
            ],
            compiler_params=params,
            cost_estimate=cost,
        )(landed, gated, wm, gq, gk, gv, taps_near)

    with jax.named_scope("close"):
        begun = [pltpu.with_memory_space_constraint(x, pltpu.HBM) for x in (oq, ok, ov)]
        block_out, grad_query, grad_key, grad_value = pl.pallas_call(
            close_kernel,
            in_specs=[vmem] * 5 + [hbm] * 3,
            out_specs=[hbm] * 4,
            out_shape=[half] * 4,
            input_output_aliases={5: 1, 6: 2, 7: 3},
            scratch_shapes=[
                pltpu.VMEM((2 * EDGE, width), f32),
                pltpu.VMEM((3, TAIL, width), bf16),
                pltpu.VMEM((rows, width), bf16),
                pltpu.SemaphoreType.DMA((4,)),
            ],
            compiler_params=params,
        )(ends, after, taps_near, mine, theirs, *begun)
    return (block_out, grad_query, grad_key, grad_value, grad_filter)


def solution(mesh):
    return jax.shard_map(
        on_device,
        mesh=mesh,
        in_specs=(
            P("ctx", "ch"),
            P("ctx", "ch"),
            P("ctx", "ch"),
            P(None, None, "ch"),
            P("ctx", "ch"),
            P("ch", None),
            P("ctx", "ch"),
        ),
        out_specs=(P("ctx", "ch"), P("ctx", "ch"), P("ctx", "ch"), P("ctx", "ch"), P("ctx", "ch")),
        check_vma=False,
    )
```

```python
import math

import jax
import jax.numpy as jnp
import ml_dtypes
import numpy as np
from jax import lax
from jax.experimental import pallas as pl
from jax.experimental.pallas import tpu as pltpu
from jax.sharding import PartitionSpec as P

f32 = jnp.float32
bf16 = jnp.bfloat16
EDGE = 8
TAIL = 16
WIDE = 256
LANES = 128
VMEM_LIMIT = 24 * 1024 * 1024


def shifted(value, axis, steps):
    count = lax.axis_size(axis)
    first, last = (max(0, -steps), min(count, count - steps))
    return lax.ppermute(value, axis, [(source, source + steps) for source in range(first, last)])


def halves(table):
    high = table.astype(ml_dtypes.bfloat16)
    low = (table - high.astype(np.float64)).astype(ml_dtypes.bfloat16)
    return high, low


def ring_order(parts):
    length = math.gcd(parts, 8)
    ring = [place for place in (0, 4, 2, 6, 1, 5, 3, 7) if place < length]
    plane = parts // length
    return [place * plane + spot for spot in range(plane) for place in ring]


def tables(parts, rows, gain, order):
    freqs = np.arange(parts) + 0.5
    blocks = np.asarray(order)
    inner = np.arange(rows)
    outer = np.outer(freqs, blocks) * (-2.0 * math.pi / (2 * parts))
    turn = np.outer(freqs, inner) * (-2.0 * math.pi / (2 * parts * rows))
    small = np.outer(inner, inner) % rows * (-2.0 * math.pi / rows)
    first = halves(np.concatenate([np.cos(outer), np.sin(outer)], 0))
    first = np.concatenate(first, 1)
    c, s = np.cos(small), np.sin(small)
    high, low = halves(np.block([[c, s], [-s, c]]))
    second = np.stack([high, low])
    high, low = halves(np.block([[c, -s], [s, c]]))
    back = np.stack([high, low])
    high, low = halves(np.concatenate([np.cos(outer).T, np.sin(outer).T], 1) * gain)
    last = np.concatenate([high, low], 0)
    twist = np.stack([np.cos(turn), np.sin(turn)]).astype(np.float32)
    return first, second, back, last, twist


def split(value):
    high = value.astype(bf16)
    low = (value - high.astype(f32)).astype(bf16)
    return high, low


def tails_kernel(q, k, v, out, near, sems):
    rows = q.shape[0]
    copies = [
        pltpu.make_async_copy(x.at[pl.ds(rows - TAIL, TAIL), :], near.at[which], sems.at[which])
        for which, x in enumerate((q, k, v))
    ]
    for copy in copies:
        copy.start()
    for which, copy in enumerate(copies):
        copy.wait()
        out[which] = near[which].astype(f32)[TAIL - EDGE :, :].astype(bf16)


ACROSS = (((1,), (1,)), ((), ()))


def fetch_kernel(
    here, q, k, v, filt, mine, w, taps_in, qs, ks, vs, gg, ft, wm, wo, taps, qb, kb, vb, fb, mb, pad, sems
):
    rows, width = q.shape
    half = w.shape[1] // 2
    me = here[0]
    w_mine = w.at[:, pl.ds(pl.multiple_of(me * half, half), half)]
    w_other = w.at[:, pl.ds(pl.multiple_of((1 - me) * half, half), half)]
    pairs = ((taps_in, taps), (q, qb), (k, kb), (v, vb), (filt, fb), (mine, mb), (w_mine, wm), (w_other, wo))
    copies = [pltpu.make_async_copy(src, dst, sems.at[i]) for i, (src, dst) in enumerate(pairs)]
    for copy in copies:
        copy.start()
    pad[0:EDGE, :] = jnp.zeros((EDGE, LANES), f32)
    copies[0].wait()
    for which, (buf, out) in enumerate(((qb, qs), (kb, ks), (vb, vs))):
        copies[1 + which].wait()
        for first in range(0, width, LANES):
            columns = slice(first, first + LANES)
            pad[EDGE : EDGE + rows, :] = buf[:, columns].astype(f32)
            total = taps[which, 0:1, columns] * pad[EDGE : EDGE + rows, :]
            for shift in range(1, taps.shape[1]):
                moved = pad[EDGE - shift : EDGE - shift + rows, :]
                total = total + taps[which, shift : shift + 1, columns] * moved
            out[:, columns] = total
    copies[4].wait()
    for first in range(0, width, WIDE):
        ft[first : first + WIDE, :] = fb[:, first : first + WIDE].T
    copies[5].wait()
    copies[6].wait()
    for first in range(0, width, WIDE):
        part = slice(first, first + WIDE)
        gg[:, part] = lax.dot_general(mb[...], wm[part, :], ACROSS, preferred_element_type=f32)
    copies[7].wait()


def prepare_kernel(halo, taps, qs_in, ks_in, vs_in, gg_in, ft, other, wo, send, qs, ks, vs, gg, pad):
    rows, width = gg.shape
    parts, lines, _ = send.shape
    group = lines // 3
    pad[EDGE : 2 * EDGE, :] = jnp.zeros((EDGE, WIDE), f32)
    for first in range(0, width, WIDE):
        part = slice(first, first + WIDE)
        grad = gg_in[:, part] + lax.dot_general(other[...], wo[part, :], ACROSS, preferred_element_type=f32)
        gg[:, part] = grad
        shorts = []
        for which, (before, after) in enumerate(((qs_in, qs), (ks_in, ks), (vs_in, vs))):
            pad[0:EDGE, :] = halo[which, :, part].astype(f32)
            top = before[0:EDGE, part]
            for shift in range(1, taps.shape[1]):
                top = top + taps[which, shift : shift + 1, part] * pad[EDGE - shift : 2 * EDGE - shift, :]
            value = jnp.concatenate([top, before[EDGE:, part]], 0)
            after[:, part] = value
            shorts.append(value)
        mixed = (shorts[1] * shorts[2]).T
        grad_long = (grad * shorts[0]).T
        turned = [field.reshape(WIDE // group, group, rows) for field in (mixed, ft[part, :], grad_long)]
        send[first // group : (first + WIDE) // group] = jnp.concatenate(turned, axis=1).astype(bf16)


BATCH = 4


def spectral_kernel(x, first, second, back, last, twist, out, buf):
    parts, lines, rows = x.shape
    group = lines // 3
    buf[...] = x[...].astype(f32).reshape(parts * lines, rows)
    cos, sin = twist[0], twist[1]

    def dot(left, right):
        return jnp.dot(left, right, preferred_element_type=f32)

    def wide(value, table):
        high, low = split(value)
        count = value.shape[0]
        both = dot(jnp.concatenate([high, low], 0), table[0])
        return both[:count] + both[count:] + dot(high, table[1])

    def spot(f, c):
        return pl.ds(f * group + c, parts, stride=lines)

    for base in range(0, group, BATCH):
        lanes = range(base, min(base + BATCH, group))
        turned = []
        for c in lanes:
            field = jnp.concatenate([buf[spot(f, c), :] for f in range(3)], 1).astype(bf16)
            half = dot(first[...], jnp.concatenate([field, field], 0))
            for f in range(3):
                re = half[:parts, f * rows : (f + 1) * rows]
                im = half[parts:, f * rows : (f + 1) * rows]
                turned.append(jnp.concatenate([re * cos - im * sin, re * sin + im * cos], 1))
        spec = wide(jnp.concatenate(turned, 0), second)
        solved = []
        for i in range(len(lanes)):
            (xr, xi), (kr, ki), (gr, gi) = [
                (spec[f * parts : (f + 1) * parts, :rows], spec[f * parts : (f + 1) * parts, rows:])
                for f in range(3 * i, 3 * i + 3)
            ]
            solved.append(jnp.concatenate([xr * kr - xi * ki, xr * ki + xi * kr], 1))
            solved.append(jnp.concatenate([kr * gr + ki * gi, kr * gi - ki * gr], 1))
            solved.append(jnp.concatenate([xr * gr + xi * gi, xr * gi - xi * gr], 1))
        part = wide(jnp.concatenate(solved, 0), back)
        turned = []
        for f in range(3 * len(lanes)):
            re = part[f * parts : (f + 1) * parts, :rows]
            im = part[f * parts : (f + 1) * parts, rows:]
            turned.append(jnp.concatenate([re * cos + im * sin, im * cos - re * sin], 0))
        high, low = split(jnp.concatenate(turned, 1))
        both = dot(last[...], high)
        result = both[:parts] + both[parts:] + dot(last[:parts, :], low)
        for i, c in enumerate(lanes):
            for f in range(3):
                place = (3 * i + f) * rows
                buf[spot(f, c), :] = result[:, place : place + rows]
    out[...] = buf[...].reshape(parts, lines, rows).astype(bf16)


def gate_kernel(landed, qs, ks, vs, gg, wo, gq, gk, gv, heads, gated, other):
    rows, width = qs.shape
    parts, lines, _ = landed.shape
    group = lines // 3
    for first in range(0, width, WIDE):
        part = slice(first, first + WIDE)
        values = landed[first // group : (first + WIDE) // group].astype(f32)
        long_out, grad_mixed = [
            values[:, f * group : (f + 1) * group, :].reshape(WIDE, rows).T for f in range(2)
        ]
        gated[:, part] = (qs[:, part] * long_out).astype(bf16)
        for which, (to, value) in enumerate(
            (
                (gq, gg[:, part] * long_out),
                (gk, grad_mixed * vs[:, part]),
                (gv, grad_mixed * ks[:, part]),
            )
        ):
            to[:, part] = value
            heads[which, :, part] = value[:EDGE, :].astype(bf16)
    for first in range(0, width, WIDE):
        part = slice(first, first + WIDE)
        other[:, part] = jnp.dot(gated[...], wo[:, part], preferred_element_type=f32)


def project_kernel(
    landed, gated, wm, gq, gk, gv, taps, gf, mine, ends, oq, ok, ov, pad, turned, rounded, sems
):
    rows, width = gated.shape
    parts, lines, _ = landed.shape
    group = lines // 3
    for first in range(0, width, WIDE):
        part = slice(first, first + WIDE)
        values = landed[first // group : (first + WIDE) // group].astype(f32)
        turned[:, part] = values[:, 2 * group :, :].reshape(WIDE, rows).T
    copies = [pltpu.make_async_copy(turned, gf, sems.at[3])]
    copies[0].start()
    pad[rows : rows + EDGE, :] = jnp.zeros((EDGE, LANES), f32)
    for which, (value, to) in enumerate(((gq, oq), (gk, ok), (gv, ov))):
        for first in range(0, width, LANES):
            part = slice(first, first + LANES)
            pad[0:rows, :] = value[:, part]
            total = taps[which, 0:1, part] * value[:, part]
            for shift in range(1, taps.shape[1]):
                total = total + taps[which, shift : shift + 1, part] * pad[shift : shift + rows, :]
            rounded[which, :, part] = total.astype(bf16)
            ends[which, :, part] = total[rows - TAIL :, :]
        copy = pltpu.make_async_copy(rounded.at[which], to, sems.at[which])
        copy.start()
        copies.append(copy)
    for first in range(0, width, WIDE):
        part = slice(first, first + WIDE)
        mine[:, part] = jnp.dot(gated[...], wm[:, part], preferred_element_type=f32)
    for copy in copies:
        copy.wait()


def close_kernel(
    ends, after, taps, mine, other, near_q, near_k, near_v, block_out, oq, ok, ov, pad, tail, total, sems
):
    rows, width = mine.shape
    total[...] = (mine[...] + other[...]).astype(bf16)
    copies = [pltpu.make_async_copy(total, block_out, sems.at[3])]
    copies[0].start()
    pad[0:EDGE, :] = jnp.zeros((EDGE, width), f32)
    for which, to in enumerate((oq, ok, ov)):
        pad[EDGE : 2 * EDGE, :] = after[which].astype(f32)
        end = ends[which, TAIL - EDGE :, :]
        for shift in range(1, taps.shape[1]):
            end = end + taps[which, shift : shift + 1, :] * pad[shift : shift + EDGE, :]
        tail[which] = jnp.concatenate([ends[which, : TAIL - EDGE, :], end], 0).astype(bf16)
        copy = pltpu.make_async_copy(tail.at[which], to.at[pl.ds(rows - TAIL, TAIL), :], sems.at[which])
        copy.start()
        copies.append(copy)
    for copy in copies:
        copy.wait()


def on_device(query_in, key_in, value_in, taps, long_filter, out_weight, out_grad):
    rows, width = query_in.shape
    parts = lax.axis_size("ctx")
    seq_total = parts * rows
    group = width // parts
    lines = 3 * group
    outs = out_weight.shape[1]
    here = lax.axis_index("ch").astype(jnp.int32).reshape(1)
    gain = 1.0 / math.sqrt(seq_total) / seq_total
    swap = [(0, 1), (1, 0)]
    order = ring_order(parts)

    params = pltpu.CompilerParams(vmem_limit_bytes=VMEM_LIMIT)
    vmem = pl.BlockSpec(memory_space=pltpu.VMEM)
    hbm = pl.BlockSpec(memory_space=pltpu.HBM)
    smem = pl.BlockSpec(memory_space=pltpu.SMEM)
    flat = jax.ShapeDtypeStruct((rows, width), f32)
    half = jax.ShapeDtypeStruct((rows, width), bf16)
    fields = jax.ShapeDtypeStruct((parts, lines, rows), bf16)
    edges = jax.ShapeDtypeStruct((3, EDGE, width), bf16)
    weights = jax.ShapeDtypeStruct((width, outs // 2), bf16)
    cost = pl.CostEstimate(flops=2 * rows * width * outs, bytes_accessed=8 * 2**20, transcendentals=0)

    grad_other = lax.ppermute(out_grad, "ch", swap)
    far = [
        pltpu.with_memory_space_constraint(x, pltpu.HBM)
        for x in (query_in, key_in, value_in, long_filter, out_grad, out_weight, taps)
    ]
    with jax.named_scope("tails"):
        tails = pl.pallas_call(
            tails_kernel,
            in_specs=[hbm] * 3,
            out_specs=vmem,
            out_shape=edges,
            scratch_shapes=[pltpu.VMEM((3, TAIL, width), bf16), pltpu.SemaphoreType.DMA((3,))],
            compiler_params=params,
        )(*far[:3])
    halo = shifted(tails, "ctx", 1)

    with jax.named_scope("fetch"):
        qs, ks, vs, gg, ft, wm, wo, taps_near = pl.pallas_call(
            fetch_kernel,
            in_specs=[smem] + [hbm] * 7,
            out_specs=[vmem] * 8,
            out_shape=[
                flat,
                flat,
                flat,
                flat,
                jax.ShapeDtypeStruct((width, rows), f32),
                weights,
                weights,
                jax.ShapeDtypeStruct(taps.shape, f32),
            ],
            scratch_shapes=[
                pltpu.VMEM((rows, width), bf16),
                pltpu.VMEM((rows, width), bf16),
                pltpu.VMEM((rows, width), bf16),
                pltpu.VMEM((rows, width), f32),
                pltpu.VMEM((rows, width), bf16),
                pltpu.VMEM((rows + EDGE, LANES), f32),
                pltpu.SemaphoreType.DMA((8,)),
            ],
            compiler_params=params,
            cost_estimate=cost,
        )(here, *far)

    with jax.named_scope("prepare"):
        send, qs, ks, vs, gg = pl.pallas_call(
            prepare_kernel,
            in_specs=[vmem] * 9,
            out_specs=[vmem] * 5,
            out_shape=[fields, flat, flat, flat, flat],
            scratch_shapes=[pltpu.VMEM((2 * EDGE, WIDE), f32)],
            compiler_params=params,
        )(halo, taps_near, qs, ks, vs, gg, ft, grad_other, wo)

    arrived = lax.all_to_all(
        send, "ctx", split_axis=0, concat_axis=0, tiled=True, axis_index_groups=[order]
    )

    with jax.named_scope("spectral"):
        solved = pl.pallas_call(
            spectral_kernel,
            out_shape=fields,
            scratch_shapes=[pltpu.VMEM((parts * lines, rows), f32)],
            compiler_params=params,
        )(arrived, *tables(parts, rows, gain, order))

    landed = lax.all_to_all(
        solved, "ctx", split_axis=0, concat_axis=0, tiled=True, axis_index_groups=[order]
    )

    with jax.named_scope("gate"):
        gq, gk, gv, heads, gated, other = pl.pallas_call(
            gate_kernel,
            in_specs=[vmem] * 6,
            out_specs=[vmem] * 6,
            out_shape=[flat, flat, flat, edges, half, flat],
            compiler_params=params,
        )(landed, qs, ks, vs, gg, wo)

    after = shifted(heads, "ctx", -1)
    theirs = lax.ppermute(other, "ch", swap)

    with jax.named_scope("project"):
        grad_filter, mine, ends, oq, ok, ov = pl.pallas_call(
            project_kernel,
            in_specs=[vmem] * 7,
            out_specs=[hbm, vmem, vmem, hbm, hbm, hbm],
            out_shape=[flat, flat, jax.ShapeDtypeStruct((3, TAIL, width), f32), half, half, half],
            scratch_shapes=[
                pltpu.VMEM((rows + EDGE, LANES), f32),
                pltpu.VMEM((rows, width), f32),
                pltpu.VMEM((3, rows, width), bf16),
                pltpu.SemaphoreType.DMA((4,)),
            ],
            compiler_params=params,
            cost_estimate=cost,
        )(landed, gated, wm, gq, gk, gv, taps_near)

    with jax.named_scope("close"):
        begun = [pltpu.with_memory_space_constraint(x, pltpu.HBM) for x in (oq, ok, ov)]
        block_out, grad_query, grad_key, grad_value = pl.pallas_call(
            close_kernel,
            in_specs=[vmem] * 5 + [hbm] * 3,
            out_specs=[hbm] * 4,
            out_shape=[half] * 4,
            input_output_aliases={5: 1, 6: 2, 7: 3},
            scratch_shapes=[
                pltpu.VMEM((2 * EDGE, width), f32),
                pltpu.VMEM((3, TAIL, width), bf16),
                pltpu.VMEM((rows, width), bf16),
                pltpu.SemaphoreType.DMA((4,)),
            ],
            compiler_params=params,
        )(ends, after, taps_near, mine, theirs, *begun)
    return (block_out, grad_query, grad_key, grad_value, grad_filter)


def solution(mesh):
    return jax.shard_map(
        on_device,
        mesh=mesh,
        in_specs=(
            P("ctx", "ch"),
            P("ctx", "ch"),
            P("ctx", "ch"),
            P(None, None, "ch"),
            P("ctx", "ch"),
            P("ch", None),
            P("ctx", "ch"),
        ),
        out_specs=(P("ctx", "ch"), P("ctx", "ch"), P("ctx", "ch"), P("ctx", "ch"), P("ctx", "ch")),
        check_vma=False,
    )
```

```python
import math

import jax
import jax.numpy as jnp
import ml_dtypes
import numpy as np
from jax import lax
from jax.experimental import pallas as pl
from jax.experimental.pallas import tpu as pltpu
from jax.sharding import PartitionSpec as P

f32 = jnp.float32
bf16 = jnp.bfloat16
EDGE = 8
TAIL = 16
WIDE = 256
LANES = 128
VMEM_LIMIT = 24 * 1024 * 1024


def shifted(value, axis, steps):
    count = lax.axis_size(axis)
    first, last = (max(0, -steps), min(count, count - steps))
    return lax.ppermute(value, axis, [(source, source + steps) for source in range(first, last)])


def halves(table):
    high = table.astype(ml_dtypes.bfloat16)
    low = (table - high.astype(np.float64)).astype(ml_dtypes.bfloat16)
    return high, low


def ring_order(parts):
    length = math.gcd(parts, 8)
    ring = [place for place in (0, 4, 2, 6, 1, 5, 3, 7) if place < length]
    plane = parts // length
    return [place * plane + spot for spot in range(plane) for place in ring]


def tables(parts, rows, gain, order):
    freqs = np.arange(parts) + 0.5
    blocks = np.asarray(order)
    inner = np.arange(rows)
    outer = np.outer(freqs, blocks) * (-2.0 * math.pi / (2 * parts))
    turn = np.outer(freqs, inner) * (-2.0 * math.pi / (2 * parts * rows))
    small = np.outer(inner, inner) % rows * (-2.0 * math.pi / rows)
    first = halves(np.concatenate([np.cos(outer), np.sin(outer)], 0))
    first = np.concatenate(first, 1)
    c, s = np.cos(small), np.sin(small)
    high, low = halves(np.block([[c, s], [-s, c]]))
    second = np.stack([high, low])
    high, low = halves(np.block([[c, -s], [s, c]]))
    back = np.stack([high, low])
    high, low = halves(np.concatenate([np.cos(outer).T, np.sin(outer).T], 1) * gain)
    last = np.concatenate([high, low], 0)
    twist = np.stack([np.cos(turn), np.sin(turn)]).astype(np.float32)
    return first, second, back, last, twist


def split(value):
    high = value.astype(bf16)
    low = (value - high.astype(f32)).astype(bf16)
    return high, low


def tails_kernel(q, k, v, out, near, sems):
    rows = q.shape[0]
    copies = [
        pltpu.make_async_copy(x.at[pl.ds(rows - TAIL, TAIL), :], near.at[which], sems.at[which])
        for which, x in enumerate((q, k, v))
    ]
    for copy in copies:
        copy.start()
    for which, copy in enumerate(copies):
        copy.wait()
        out[which] = near[which].astype(f32)[TAIL - EDGE :, :].astype(bf16)


ACROSS = (((1,), (1,)), ((), ()))


def fetch_kernel(
    here, q, k, v, filt, mine, w, taps_in, qs, ks, vs, gg, ft, wm, wo, taps, qb, kb, vb, fb, mb, pad, sems
):
    rows, width = q.shape
    half = w.shape[1] // 2
    me = here[0]
    w_mine = w.at[:, pl.ds(pl.multiple_of(me * half, half), half)]
    w_other = w.at[:, pl.ds(pl.multiple_of((1 - me) * half, half), half)]
    pairs = ((taps_in, taps), (q, qb), (k, kb), (v, vb), (filt, fb), (mine, mb), (w_mine, wm), (w_other, wo))
    copies = [pltpu.make_async_copy(src, dst, sems.at[i]) for i, (src, dst) in enumerate(pairs)]
    for copy in copies:
        copy.start()
    pad[0:EDGE, :] = jnp.zeros((EDGE, LANES), f32)
    copies[0].wait()
    for which, (buf, out) in enumerate(((qb, qs), (kb, ks), (vb, vs))):
        copies[1 + which].wait()
        for first in range(0, width, LANES):
            columns = slice(first, first + LANES)
            pad[EDGE : EDGE + rows, :] = buf[:, columns].astype(f32)
            total = taps[which, 0:1, columns] * pad[EDGE : EDGE + rows, :]
            for shift in range(1, taps.shape[1]):
                moved = pad[EDGE - shift : EDGE - shift + rows, :]
                total = total + taps[which, shift : shift + 1, columns] * moved
            out[:, columns] = total
    copies[4].wait()
    for first in range(0, width, WIDE):
        ft[first : first + WIDE, :] = fb[:, first : first + WIDE].T
    copies[5].wait()
    copies[6].wait()
    for first in range(0, width, WIDE):
        part = slice(first, first + WIDE)
        gg[:, part] = lax.dot_general(mb[...], wm[part, :], ACROSS, preferred_element_type=f32)
    copies[7].wait()


def prepare_kernel(halo, taps, qs_in, ks_in, vs_in, gg_in, ft, other, wo, send, qs, ks, vs, gg, pad):
    rows, width = gg.shape
    parts, lines, _ = send.shape
    group = lines // 3
    pad[EDGE : 2 * EDGE, :] = jnp.zeros((EDGE, WIDE), f32)
    for first in range(0, width, WIDE):
        part = slice(first, first + WIDE)
        grad = gg_in[:, part] + lax.dot_general(other[...], wo[part, :], ACROSS, preferred_element_type=f32)
        gg[:, part] = grad
        shorts = []
        for which, (before, after) in enumerate(((qs_in, qs), (ks_in, ks), (vs_in, vs))):
            pad[0:EDGE, :] = halo[which, :, part].astype(f32)
            top = before[0:EDGE, part]
            for shift in range(1, taps.shape[1]):
                top = top + taps[which, shift : shift + 1, part] * pad[EDGE - shift : 2 * EDGE - shift, :]
            value = jnp.concatenate([top, before[EDGE:, part]], 0)
            after[:, part] = value
            shorts.append(value)
        mixed = (shorts[1] * shorts[2]).T
        grad_long = (grad * shorts[0]).T
        turned = [field.reshape(WIDE // group, group, rows) for field in (mixed, ft[part, :], grad_long)]
        send[first // group : (first + WIDE) // group] = jnp.concatenate(turned, axis=1).astype(bf16)


BATCH = 4


def spectral_kernel(x, first, second, back, last, twist, out, buf):
    parts, lines, rows = x.shape
    group = lines // 3
    buf[...] = x[...].astype(f32).reshape(parts * lines, rows)
    cos, sin = twist[0], twist[1]

    def dot(left, right):
        return jnp.dot(left, right, preferred_element_type=f32)

    def wide(value, table):
        high, low = split(value)
        count = value.shape[0]
        both = dot(jnp.concatenate([high, low], 0), table[0])
        return both[:count] + both[count:] + dot(high, table[1])

    def spot(f, c):
        return pl.ds(f * group + c, parts, stride=lines)

    for base in range(0, group, BATCH):
        lanes = range(base, min(base + BATCH, group))
        turned = []
        for c in lanes:
            field = jnp.concatenate([buf[spot(f, c), :] for f in range(3)], 1).astype(bf16)
            half = dot(first[...], jnp.concatenate([field, field], 0))
            for f in range(3):
                re = half[:parts, f * rows : (f + 1) * rows]
                im = half[parts:, f * rows : (f + 1) * rows]
                turned.append(jnp.concatenate([re * cos - im * sin, re * sin + im * cos], 1))
        spec = wide(jnp.concatenate(turned, 0), second)
        solved = []
        for i in range(len(lanes)):
            (xr, xi), (kr, ki), (gr, gi) = [
                (spec[f * parts : (f + 1) * parts, :rows], spec[f * parts : (f + 1) * parts, rows:])
                for f in range(3 * i, 3 * i + 3)
            ]
            solved.append(jnp.concatenate([xr * kr - xi * ki, xr * ki + xi * kr], 1))
            solved.append(jnp.concatenate([kr * gr + ki * gi, kr * gi - ki * gr], 1))
            solved.append(jnp.concatenate([xr * gr + xi * gi, xr * gi - xi * gr], 1))
        part = wide(jnp.concatenate(solved, 0), back)
        turned = []
        for f in range(3 * len(lanes)):
            re = part[f * parts : (f + 1) * parts, :rows]
            im = part[f * parts : (f + 1) * parts, rows:]
            turned.append(jnp.concatenate([re * cos + im * sin, im * cos - re * sin], 0))
        high, low = split(jnp.concatenate(turned, 1))
        both = dot(last[...], high)
        result = both[:parts] + both[parts:] + dot(last[:parts, :], low)
        for i, c in enumerate(lanes):
            for f in range(3):
                place = (3 * i + f) * rows
                buf[spot(f, c), :] = result[:, place : place + rows]
    out[...] = buf[...].reshape(parts, lines, rows).astype(bf16)


def gate_kernel(landed, qs, ks, vs, gg, wo, gq, gk, gv, heads, gated, other):
    rows, width = qs.shape
    parts, lines, _ = landed.shape
    group = lines // 3
    for first in range(0, width, WIDE):
        part = slice(first, first + WIDE)
        values = landed[first // group : (first + WIDE) // group].astype(f32)
        long_out, grad_mixed = [
            values[:, f * group : (f + 1) * group, :].reshape(WIDE, rows).T for f in range(2)
        ]
        gated[:, part] = (qs[:, part] * long_out).astype(bf16)
        for which, (to, value) in enumerate(
            (
                (gq, gg[:, part] * long_out),
                (gk, grad_mixed * vs[:, part]),
                (gv, grad_mixed * ks[:, part]),
            )
        ):
            to[:, part] = value
            heads[which, :, part] = value[:EDGE, :].astype(bf16)
    for first in range(0, width, WIDE):
        part = slice(first, first + WIDE)
        other[:, part] = jnp.dot(gated[...], wo[:, part], preferred_element_type=f32)


def project_kernel(
    landed, gated, wm, gq, gk, gv, taps, gf, mine, ends, oq, ok, ov, pad, turned, rounded, sems
):
    rows, width = gated.shape
    parts, lines, _ = landed.shape
    group = lines // 3
    for first in range(0, width, WIDE):
        part = slice(first, first + WIDE)
        values = landed[first // group : (first + WIDE) // group].astype(f32)
        turned[:, part] = values[:, 2 * group :, :].reshape(WIDE, rows).T
    copies = [pltpu.make_async_copy(turned, gf, sems.at[3])]
    copies[0].start()
    pad[rows : rows + EDGE, :] = jnp.zeros((EDGE, LANES), f32)
    for which, (value, to) in enumerate(((gq, oq), (gk, ok), (gv, ov))):
        for first in range(0, width, LANES):
            part = slice(first, first + LANES)
            pad[0:rows, :] = value[:, part]
            total = taps[which, 0:1, part] * value[:, part]
            for shift in range(1, taps.shape[1]):
                total = total + taps[which, shift : shift + 1, part] * pad[shift : shift + rows, :]
            rounded[which, :, part] = total.astype(bf16)
            ends[which, :, part] = total[rows - TAIL :, :]
        copy = pltpu.make_async_copy(rounded.at[which], to, sems.at[which])
        copy.start()
        copies.append(copy)
    for first in range(0, width, WIDE):
        part = slice(first, first + WIDE)
        mine[:, part] = jnp.dot(gated[...], wm[:, part], preferred_element_type=f32)
    for copy in copies:
        copy.wait()


def close_kernel(
    ends, after, taps, mine, other, near_q, near_k, near_v, block_out, oq, ok, ov, pad, tail, total, sems
):
    rows, width = mine.shape
    total[...] = (mine[...] + other[...]).astype(bf16)
    copies = [pltpu.make_async_copy(total, block_out, sems.at[3])]
    copies[0].start()
    pad[0:EDGE, :] = jnp.zeros((EDGE, width), f32)
    for which, to in enumerate((oq, ok, ov)):
        pad[EDGE : 2 * EDGE, :] = after[which].astype(f32)
        end = ends[which, TAIL - EDGE :, :]
        for shift in range(1, taps.shape[1]):
            end = end + taps[which, shift : shift + 1, :] * pad[shift : shift + EDGE, :]
        tail[which] = jnp.concatenate([ends[which, : TAIL - EDGE, :], end], 0).astype(bf16)
        copy = pltpu.make_async_copy(tail.at[which], to.at[pl.ds(rows - TAIL, TAIL), :], sems.at[which])
        copy.start()
        copies.append(copy)
    for copy in copies:
        copy.wait()


def on_device(query_in, key_in, value_in, taps, long_filter, out_weight, out_grad):
    rows, width = query_in.shape
    parts = lax.axis_size("ctx")
    seq_total = parts * rows
    group = width // parts
    lines = 3 * group
    outs = out_weight.shape[1]
    here = lax.axis_index("ch").astype(jnp.int32).reshape(1)
    gain = 1.0 / math.sqrt(seq_total) / seq_total
    swap = [(0, 1), (1, 0)]
    order = ring_order(parts)

    params = pltpu.CompilerParams(vmem_limit_bytes=VMEM_LIMIT)
    vmem = pl.BlockSpec(memory_space=pltpu.VMEM)
    hbm = pl.BlockSpec(memory_space=pltpu.HBM)
    smem = pl.BlockSpec(memory_space=pltpu.SMEM)
    flat = jax.ShapeDtypeStruct((rows, width), f32)
    half = jax.ShapeDtypeStruct((rows, width), bf16)
    fields = jax.ShapeDtypeStruct((parts, lines, rows), bf16)
    edges = jax.ShapeDtypeStruct((3, EDGE, width), bf16)
    weights = jax.ShapeDtypeStruct((width, outs // 2), bf16)
    cost = pl.CostEstimate(flops=2 * rows * width * outs, bytes_accessed=8 * 2**20, transcendentals=0)

    grad_other = lax.ppermute(out_grad, "ch", swap)
    far = [
        pltpu.with_memory_space_constraint(x, pltpu.HBM)
        for x in (query_in, key_in, value_in, long_filter, out_grad, out_weight, taps)
    ]
    with jax.named_scope("tails"):
        tails = pl.pallas_call(
            tails_kernel,
            in_specs=[hbm] * 3,
            out_specs=vmem,
            out_shape=edges,
            scratch_shapes=[pltpu.VMEM((3, TAIL, width), bf16), pltpu.SemaphoreType.DMA((3,))],
            compiler_params=params,
        )(*far[:3])
    halo = shifted(tails, "ctx", 1)

    with jax.named_scope("fetch"):
        qs, ks, vs, gg, ft, wm, wo, taps_near = pl.pallas_call(
            fetch_kernel,
            in_specs=[smem] + [hbm] * 7,
            out_specs=[vmem] * 8,
            out_shape=[
                flat,
                flat,
                flat,
                flat,
                jax.ShapeDtypeStruct((width, rows), f32),
                weights,
                weights,
                jax.ShapeDtypeStruct(taps.shape, f32),
            ],
            scratch_shapes=[
                pltpu.VMEM((rows, width), bf16),
                pltpu.VMEM((rows, width), bf16),
                pltpu.VMEM((rows, width), bf16),
                pltpu.VMEM((rows, width), f32),
                pltpu.VMEM((rows, width), bf16),
                pltpu.VMEM((rows + EDGE, LANES), f32),
                pltpu.SemaphoreType.DMA((8,)),
            ],
            compiler_params=params,
            cost_estimate=cost,
        )(here, *far)

    with jax.named_scope("prepare"):
        send, qs, ks, vs, gg = pl.pallas_call(
            prepare_kernel,
            in_specs=[vmem] * 9,
            out_specs=[vmem] * 5,
            out_shape=[fields, flat, flat, flat, flat],
            scratch_shapes=[pltpu.VMEM((2 * EDGE, WIDE), f32)],
            compiler_params=params,
        )(halo, taps_near, qs, ks, vs, gg, ft, grad_other, wo)

    send = pltpu.with_memory_space_constraint(send, pltpu.HBM)
    arrived = lax.all_to_all(
        send, "ctx", split_axis=0, concat_axis=0, tiled=True, axis_index_groups=[order]
    )

    with jax.named_scope("spectral"):
        solved = pl.pallas_call(
            spectral_kernel,
            out_shape=fields,
            scratch_shapes=[pltpu.VMEM((parts * lines, rows), f32)],
            compiler_params=params,
        )(arrived, *tables(parts, rows, gain, order))

    solved = pltpu.with_memory_space_constraint(solved, pltpu.HBM)
    landed = lax.all_to_all(
        solved, "ctx", split_axis=0, concat_axis=0, tiled=True, axis_index_groups=[order]
    )

    with jax.named_scope("gate"):
        gq, gk, gv, heads, gated, other = pl.pallas_call(
            gate_kernel,
            in_specs=[vmem] * 6,
            out_specs=[vmem] * 6,
            out_shape=[flat, flat, flat, edges, half, flat],
            compiler_params=params,
        )(landed, qs, ks, vs, gg, wo)

    after = shifted(heads, "ctx", -1)
    theirs = lax.ppermute(other, "ch", swap)

    with jax.named_scope("project"):
        grad_filter, mine, ends, oq, ok, ov = pl.pallas_call(
            project_kernel,
            in_specs=[vmem] * 7,
            out_specs=[hbm, vmem, vmem, hbm, hbm, hbm],
            out_shape=[flat, flat, jax.ShapeDtypeStruct((3, TAIL, width), f32), half, half, half],
            scratch_shapes=[
                pltpu.VMEM((rows + EDGE, LANES), f32),
                pltpu.VMEM((rows, width), f32),
                pltpu.VMEM((3, rows, width), bf16),
                pltpu.SemaphoreType.DMA((4,)),
            ],
            compiler_params=params,
            cost_estimate=cost,
        )(landed, gated, wm, gq, gk, gv, taps_near)

    with jax.named_scope("close"):
        begun = [pltpu.with_memory_space_constraint(x, pltpu.HBM) for x in (oq, ok, ov)]
        block_out, grad_query, grad_key, grad_value = pl.pallas_call(
            close_kernel,
            in_specs=[vmem] * 5 + [hbm] * 3,
            out_specs=[hbm] * 4,
            out_shape=[half] * 4,
            input_output_aliases={5: 1, 6: 2, 7: 3},
            scratch_shapes=[
                pltpu.VMEM((2 * EDGE, width), f32),
                pltpu.VMEM((3, TAIL, width), bf16),
                pltpu.VMEM((rows, width), bf16),
                pltpu.SemaphoreType.DMA((4,)),
            ],
            compiler_params=params,
        )(ends, after, taps_near, mine, theirs, *begun)
    return (block_out, grad_query, grad_key, grad_value, grad_filter)


def solution(mesh):
    return jax.shard_map(
        on_device,
        mesh=mesh,
        in_specs=(
            P("ctx", "ch"),
            P("ctx", "ch"),
            P("ctx", "ch"),
            P(None, None, "ch"),
            P("ctx", "ch"),
            P("ch", None),
            P("ctx", "ch"),
        ),
        out_specs=(P("ctx", "ch"), P("ctx", "ch"), P("ctx", "ch"), P("ctx", "ch"), P("ctx", "ch")),
        check_vma=False,
    )
```

```python
import math

import jax
import jax.numpy as jnp
import ml_dtypes
import numpy as np
from jax import lax
from jax.experimental import pallas as pl
from jax.experimental.pallas import tpu as pltpu
from jax.sharding import PartitionSpec as P

f32 = jnp.float32
bf16 = jnp.bfloat16
EDGE = 8
TAIL = 16
WIDE = 256
LANES = 128
VMEM_LIMIT = 24 * 1024 * 1024


def shifted(value, axis, steps):
    count = lax.axis_size(axis)
    first, last = (max(0, -steps), min(count, count - steps))
    return lax.ppermute(value, axis, [(source, source + steps) for source in range(first, last)])


def halves(table):
    high = table.astype(ml_dtypes.bfloat16)
    low = (table - high.astype(np.float64)).astype(ml_dtypes.bfloat16)
    return high, low


def ring_order(parts):
    length = math.gcd(parts, 8)
    ring = [place for place in (0, 4, 2, 6, 1, 5, 3, 7) if place < length]
    plane = parts // length
    return [place * plane + spot for spot in range(plane) for place in ring]


def tables(parts, rows, gain, order):
    freqs = np.arange(parts) + 0.5
    blocks = np.asarray(order)
    inner = np.arange(rows)
    outer = np.outer(freqs, blocks) * (-2.0 * math.pi / (2 * parts))
    turn = np.outer(freqs, inner) * (-2.0 * math.pi / (2 * parts * rows))
    small = np.outer(inner, inner) % rows * (-2.0 * math.pi / rows)
    first = halves(np.concatenate([np.cos(outer), np.sin(outer)], 0))
    first = np.concatenate(first, 1)
    c, s = np.cos(small), np.sin(small)
    high, low = halves(np.block([[c, s], [-s, c]]))
    second = np.stack([high, low])
    high, low = halves(np.block([[c, -s], [s, c]]))
    back = np.stack([high, low])
    high, low = halves(np.concatenate([np.cos(outer).T, np.sin(outer).T], 1) * gain)
    last = np.concatenate([high, low], 0)
    twist = np.stack([np.cos(turn), np.sin(turn)]).astype(np.float32)
    return first, second, back, last, twist


def split(value):
    high = value.astype(bf16)
    low = (value - high.astype(f32)).astype(bf16)
    return high, low


def tails_kernel(q, k, v, out, near, sems):
    rows = q.shape[0]
    copies = [
        pltpu.make_async_copy(x.at[pl.ds(rows - TAIL, TAIL), :], near.at[which], sems.at[which])
        for which, x in enumerate((q, k, v))
    ]
    for copy in copies:
        copy.start()
    for which, copy in enumerate(copies):
        copy.wait()
        out[which] = near[which].astype(f32)[TAIL - EDGE :, :].astype(bf16)


ACROSS = (((1,), (1,)), ((), ()))


def fetch_kernel(
    here, q, k, v, filt, mine, w, taps_in, qs, ks, vs, gg, ft, wm, wo, taps, qb, kb, vb, fb, mb, pad, sems
):
    rows, width = q.shape
    half = w.shape[1] // 2
    me = here[0]
    w_mine = w.at[:, pl.ds(pl.multiple_of(me * half, half), half)]
    w_other = w.at[:, pl.ds(pl.multiple_of((1 - me) * half, half), half)]
    pairs = ((taps_in, taps), (q, qb), (k, kb), (v, vb), (filt, fb), (mine, mb), (w_mine, wm), (w_other, wo))
    copies = [pltpu.make_async_copy(src, dst, sems.at[i]) for i, (src, dst) in enumerate(pairs)]
    for copy in copies:
        copy.start()
    pad[0:EDGE, :] = jnp.zeros((EDGE, LANES), f32)
    copies[0].wait()
    for which, (buf, out) in enumerate(((qb, qs), (kb, ks), (vb, vs))):
        copies[1 + which].wait()
        for first in range(0, width, LANES):
            columns = slice(first, first + LANES)
            pad[EDGE : EDGE + rows, :] = buf[:, columns].astype(f32)
            total = taps[which, 0:1, columns] * pad[EDGE : EDGE + rows, :]
            for shift in range(1, taps.shape[1]):
                moved = pad[EDGE - shift : EDGE - shift + rows, :]
                total = total + taps[which, shift : shift + 1, columns] * moved
            out[:, columns] = total
    copies[4].wait()
    for first in range(0, width, WIDE):
        ft[first : first + WIDE, :] = fb[:, first : first + WIDE].T
    copies[5].wait()
    copies[6].wait()
    for first in range(0, width, WIDE):
        part = slice(first, first + WIDE)
        gg[:, part] = lax.dot_general(mb[...], wm[part, :], ACROSS, preferred_element_type=f32)
    copies[7].wait()


def prepare_kernel(halo, taps, qs_in, ks_in, vs_in, gg_in, ft, other, wo, send, qs, ks, vs, gg, pad):
    rows, width = gg.shape
    parts, lines, _ = send.shape
    group = lines // 3
    pad[EDGE : 2 * EDGE, :] = jnp.zeros((EDGE, WIDE), f32)
    for first in range(0, width, WIDE):
        part = slice(first, first + WIDE)
        grad = gg_in[:, part] + lax.dot_general(other[...], wo[part, :], ACROSS, preferred_element_type=f32)
        gg[:, part] = grad
        shorts = []
        for which, (before, after) in enumerate(((qs_in, qs), (ks_in, ks), (vs_in, vs))):
            pad[0:EDGE, :] = halo[which, :, part].astype(f32)
            top = before[0:EDGE, part]
            for shift in range(1, taps.shape[1]):
                top = top + taps[which, shift : shift + 1, part] * pad[EDGE - shift : 2 * EDGE - shift, :]
            value = jnp.concatenate([top, before[EDGE:, part]], 0)
            after[:, part] = value
            shorts.append(value)
        mixed = (shorts[1] * shorts[2]).T
        grad_long = (grad * shorts[0]).T
        turned = [field.reshape(WIDE // group, group, rows) for field in (mixed, ft[part, :], grad_long)]
        send[first // group : (first + WIDE) // group] = jnp.concatenate(turned, axis=1).astype(bf16)


BATCH = 8


def spectral_kernel(x, first, second, back, last, twist, out, buf):
    parts, lines, rows = x.shape
    group = lines // 3
    buf[...] = x[...].astype(f32).reshape(parts * lines, rows)
    cos, sin = twist[0], twist[1]

    def dot(left, right):
        return jnp.dot(left, right, preferred_element_type=f32)

    def wide(value, table):
        high, low = split(value)
        count = value.shape[0]
        both = dot(jnp.concatenate([high, low], 0), table[0])
        return both[:count] + both[count:] + dot(high, table[1])

    def spot(f, c):
        return pl.ds(f * group + c, parts, stride=lines)

    for base in range(0, group, BATCH):
        lanes = range(base, min(base + BATCH, group))
        turned = []
        for c in lanes:
            field = jnp.concatenate([buf[spot(f, c), :] for f in range(3)], 1).astype(bf16)
            half = dot(first[...], jnp.concatenate([field, field], 0))
            for f in range(3):
                re = half[:parts, f * rows : (f + 1) * rows]
                im = half[parts:, f * rows : (f + 1) * rows]
                turned.append(jnp.concatenate([re * cos - im * sin, re * sin + im * cos], 1))
        spec = wide(jnp.concatenate(turned, 0), second)
        solved = []
        for i in range(len(lanes)):
            (xr, xi), (kr, ki), (gr, gi) = [
                (spec[f * parts : (f + 1) * parts, :rows], spec[f * parts : (f + 1) * parts, rows:])
                for f in range(3 * i, 3 * i + 3)
            ]
            solved.append(jnp.concatenate([xr * kr - xi * ki, xr * ki + xi * kr], 1))
            solved.append(jnp.concatenate([kr * gr + ki * gi, kr * gi - ki * gr], 1))
            solved.append(jnp.concatenate([xr * gr + xi * gi, xr * gi - xi * gr], 1))
        part = wide(jnp.concatenate(solved, 0), back)
        turned = []
        for f in range(3 * len(lanes)):
            re = part[f * parts : (f + 1) * parts, :rows]
            im = part[f * parts : (f + 1) * parts, rows:]
            turned.append(jnp.concatenate([re * cos + im * sin, im * cos - re * sin], 0))
        high, low = split(jnp.concatenate(turned, 1))
        both = dot(last[...], high)
        result = both[:parts] + both[parts:] + dot(last[:parts, :], low)
        for i, c in enumerate(lanes):
            for f in range(3):
                place = (3 * i + f) * rows
                buf[spot(f, c), :] = result[:, place : place + rows]
    out[...] = buf[...].reshape(parts, lines, rows).astype(bf16)


def gate_kernel(landed, qs, ks, vs, gg, wo, gq, gk, gv, heads, gated, other):
    rows, width = qs.shape
    parts, lines, _ = landed.shape
    group = lines // 3
    for first in range(0, width, WIDE):
        part = slice(first, first + WIDE)
        values = landed[first // group : (first + WIDE) // group].astype(f32)
        long_out, grad_mixed = [
            values[:, f * group : (f + 1) * group, :].reshape(WIDE, rows).T for f in range(2)
        ]
        gated[:, part] = (qs[:, part] * long_out).astype(bf16)
        for which, (to, value) in enumerate(
            (
                (gq, gg[:, part] * long_out),
                (gk, grad_mixed * vs[:, part]),
                (gv, grad_mixed * ks[:, part]),
            )
        ):
            to[:, part] = value
            heads[which, :, part] = value[:EDGE, :].astype(bf16)
    for first in range(0, width, WIDE):
        part = slice(first, first + WIDE)
        other[:, part] = jnp.dot(gated[...], wo[:, part], preferred_element_type=f32)


def project_kernel(
    landed, gated, wm, gq, gk, gv, taps, gf, mine, ends, oq, ok, ov, pad, turned, rounded, sems
):
    rows, width = gated.shape
    parts, lines, _ = landed.shape
    group = lines // 3
    for first in range(0, width, WIDE):
        part = slice(first, first + WIDE)
        values = landed[first // group : (first + WIDE) // group].astype(f32)
        turned[:, part] = values[:, 2 * group :, :].reshape(WIDE, rows).T
    copies = [pltpu.make_async_copy(turned, gf, sems.at[3])]
    copies[0].start()
    pad[rows : rows + EDGE, :] = jnp.zeros((EDGE, LANES), f32)
    chunks = range(0, width, WIDE)
    for which, (value, to) in enumerate(((gq, oq), (gk, ok), (gv, ov))):
        for first in chunks[which::3]:
            part = slice(first, first + WIDE)
            mine[:, part] = jnp.dot(gated[...], wm[:, part], preferred_element_type=f32)
        for first in range(0, width, LANES):
            part = slice(first, first + LANES)
            pad[0:rows, :] = value[:, part]
            total = taps[which, 0:1, part] * value[:, part]
            for shift in range(1, taps.shape[1]):
                total = total + taps[which, shift : shift + 1, part] * pad[shift : shift + rows, :]
            rounded[which, :, part] = total.astype(bf16)
            ends[which, :, part] = total[rows - TAIL :, :]
        copy = pltpu.make_async_copy(rounded.at[which], to, sems.at[which])
        copy.start()
        copies.append(copy)
    for copy in copies:
        copy.wait()


def close_kernel(
    ends, after, taps, mine, other, near_q, near_k, near_v, block_out, oq, ok, ov, pad, tail, total, sems
):
    rows, width = mine.shape
    total[...] = (mine[...] + other[...]).astype(bf16)
    copies = [pltpu.make_async_copy(total, block_out, sems.at[3])]
    copies[0].start()
    pad[0:EDGE, :] = jnp.zeros((EDGE, width), f32)
    for which, to in enumerate((oq, ok, ov)):
        pad[EDGE : 2 * EDGE, :] = after[which].astype(f32)
        end = ends[which, TAIL - EDGE :, :]
        for shift in range(1, taps.shape[1]):
            end = end + taps[which, shift : shift + 1, :] * pad[shift : shift + EDGE, :]
        tail[which] = jnp.concatenate([ends[which, : TAIL - EDGE, :], end], 0).astype(bf16)
        copy = pltpu.make_async_copy(tail.at[which], to.at[pl.ds(rows - TAIL, TAIL), :], sems.at[which])
        copy.start()
        copies.append(copy)
    for copy in copies:
        copy.wait()


def on_device(query_in, key_in, value_in, taps, long_filter, out_weight, out_grad):
    rows, width = query_in.shape
    parts = lax.axis_size("ctx")
    seq_total = parts * rows
    group = width // parts
    lines = 3 * group
    outs = out_weight.shape[1]
    here = lax.axis_index("ch").astype(jnp.int32).reshape(1)
    gain = 1.0 / math.sqrt(seq_total) / seq_total
    swap = [(0, 1), (1, 0)]
    order = ring_order(parts)

    params = pltpu.CompilerParams(vmem_limit_bytes=VMEM_LIMIT)
    vmem = pl.BlockSpec(memory_space=pltpu.VMEM)
    hbm = pl.BlockSpec(memory_space=pltpu.HBM)
    smem = pl.BlockSpec(memory_space=pltpu.SMEM)
    flat = jax.ShapeDtypeStruct((rows, width), f32)
    half = jax.ShapeDtypeStruct((rows, width), bf16)
    fields = jax.ShapeDtypeStruct((parts, lines, rows), bf16)
    edges = jax.ShapeDtypeStruct((3, EDGE, width), bf16)
    weights = jax.ShapeDtypeStruct((width, outs // 2), bf16)
    cost = pl.CostEstimate(flops=2 * rows * width * outs, bytes_accessed=8 * 2**20, transcendentals=0)

    grad_other = lax.ppermute(out_grad, "ch", swap)
    far = [
        pltpu.with_memory_space_constraint(x, pltpu.HBM)
        for x in (query_in, key_in, value_in, long_filter, out_grad, out_weight, taps)
    ]
    with jax.named_scope("tails"):
        tails = pl.pallas_call(
            tails_kernel,
            in_specs=[hbm] * 3,
            out_specs=vmem,
            out_shape=edges,
            scratch_shapes=[pltpu.VMEM((3, TAIL, width), bf16), pltpu.SemaphoreType.DMA((3,))],
            compiler_params=params,
        )(*far[:3])
    halo = shifted(tails, "ctx", 1)

    with jax.named_scope("fetch"):
        qs, ks, vs, gg, ft, wm, wo, taps_near = pl.pallas_call(
            fetch_kernel,
            in_specs=[smem] + [hbm] * 7,
            out_specs=[vmem] * 8,
            out_shape=[
                flat,
                flat,
                flat,
                flat,
                jax.ShapeDtypeStruct((width, rows), f32),
                weights,
                weights,
                jax.ShapeDtypeStruct(taps.shape, f32),
            ],
            scratch_shapes=[
                pltpu.VMEM((rows, width), bf16),
                pltpu.VMEM((rows, width), bf16),
                pltpu.VMEM((rows, width), bf16),
                pltpu.VMEM((rows, width), f32),
                pltpu.VMEM((rows, width), bf16),
                pltpu.VMEM((rows + EDGE, LANES), f32),
                pltpu.SemaphoreType.DMA((8,)),
            ],
            compiler_params=params,
            cost_estimate=cost,
        )(here, *far)

    with jax.named_scope("prepare"):
        send, qs, ks, vs, gg = pl.pallas_call(
            prepare_kernel,
            in_specs=[vmem] * 9,
            out_specs=[vmem] * 5,
            out_shape=[fields, flat, flat, flat, flat],
            scratch_shapes=[pltpu.VMEM((2 * EDGE, WIDE), f32)],
            compiler_params=params,
        )(halo, taps_near, qs, ks, vs, gg, ft, grad_other, wo)

    arrived = lax.all_to_all(
        send, "ctx", split_axis=0, concat_axis=0, tiled=True, axis_index_groups=[order]
    )

    with jax.named_scope("spectral"):
        solved = pl.pallas_call(
            spectral_kernel,
            out_shape=fields,
            scratch_shapes=[pltpu.VMEM((parts * lines, rows), f32)],
            compiler_params=params,
        )(arrived, *tables(parts, rows, gain, order))

    landed = lax.all_to_all(
        solved, "ctx", split_axis=0, concat_axis=0, tiled=True, axis_index_groups=[order]
    )

    with jax.named_scope("gate"):
        gq, gk, gv, heads, gated, other = pl.pallas_call(
            gate_kernel,
            in_specs=[vmem] * 6,
            out_specs=[vmem] * 6,
            out_shape=[flat, flat, flat, edges, half, flat],
            compiler_params=params,
        )(landed, qs, ks, vs, gg, wo)

    after = shifted(heads, "ctx", -1)
    theirs = lax.ppermute(other, "ch", swap)

    with jax.named_scope("project"):
        grad_filter, mine, ends, oq, ok, ov = pl.pallas_call(
            project_kernel,
            in_specs=[vmem] * 7,
            out_specs=[hbm, vmem, vmem, hbm, hbm, hbm],
            out_shape=[flat, flat, jax.ShapeDtypeStruct((3, TAIL, width), f32), half, half, half],
            scratch_shapes=[
                pltpu.VMEM((rows + EDGE, LANES), f32),
                pltpu.VMEM((rows, width), f32),
                pltpu.VMEM((3, rows, width), bf16),
                pltpu.SemaphoreType.DMA((4,)),
            ],
            compiler_params=params,
            cost_estimate=cost,
        )(landed, gated, wm, gq, gk, gv, taps_near)

    with jax.named_scope("close"):
        begun = [pltpu.with_memory_space_constraint(x, pltpu.HBM) for x in (oq, ok, ov)]
        block_out, grad_query, grad_key, grad_value = pl.pallas_call(
            close_kernel,
            in_specs=[vmem] * 5 + [hbm] * 3,
            out_specs=[hbm] * 4,
            out_shape=[half] * 4,
            input_output_aliases={5: 1, 6: 2, 7: 3},
            scratch_shapes=[
                pltpu.VMEM((2 * EDGE, width), f32),
                pltpu.VMEM((3, TAIL, width), bf16),
                pltpu.VMEM((rows, width), bf16),
                pltpu.SemaphoreType.DMA((4,)),
            ],
            compiler_params=params,
        )(ends, after, taps_near, mine, theirs, *begun)
    return (block_out, grad_query, grad_key, grad_value, grad_filter)


def solution(mesh):
    return jax.shard_map(
        on_device,
        mesh=mesh,
        in_specs=(
            P("ctx", "ch"),
            P("ctx", "ch"),
            P("ctx", "ch"),
            P(None, None, "ch"),
            P("ctx", "ch"),
            P("ch", None),
            P("ctx", "ch"),
        ),
        out_specs=(P("ctx", "ch"), P("ctx", "ch"), P("ctx", "ch"), P("ctx", "ch"), P("ctx", "ch")),
        check_vma=False,
    )
```

```python
import math

import jax
import jax.numpy as jnp
import ml_dtypes
import numpy as np
from jax import lax
from jax.experimental import pallas as pl
from jax.experimental.pallas import tpu as pltpu
from jax.sharding import PartitionSpec as P

f32 = jnp.float32
bf16 = jnp.bfloat16
EDGE = 8
TAIL = 16
WIDE = 256
LANES = 128
VMEM_LIMIT = 24 * 1024 * 1024


def shifted(value, axis, steps):
    count = lax.axis_size(axis)
    first, last = (max(0, -steps), min(count, count - steps))
    return lax.ppermute(value, axis, [(source, source + steps) for source in range(first, last)])


def halves(table):
    high = table.astype(ml_dtypes.bfloat16)
    low = (table - high.astype(np.float64)).astype(ml_dtypes.bfloat16)
    return high, low


def ring_order(parts):
    length = math.gcd(parts, 8)
    ring = [place for place in (0, 4, 2, 6, 1, 5, 3, 7) if place < length]
    plane = parts // length
    return [place * plane + spot for spot in range(plane) for place in ring]


def tables(parts, rows, gain, order):
    freqs = np.arange(parts) + 0.5
    blocks = np.asarray(order)
    inner = np.arange(rows)
    outer = np.outer(freqs, blocks) * (-2.0 * math.pi / (2 * parts))
    turn = np.outer(freqs, inner) * (-2.0 * math.pi / (2 * parts * rows))
    small = np.outer(inner, inner) % rows * (-2.0 * math.pi / rows)
    first = halves(np.concatenate([np.cos(outer), np.sin(outer)], 0))
    first = np.concatenate(first, 1)
    c, s = np.cos(small), np.sin(small)
    high, low = halves(np.block([[c, s], [-s, c]]))
    second = np.stack([high, low])
    high, low = halves(np.block([[c, -s], [s, c]]))
    back = np.stack([high, low])
    high, low = halves(np.concatenate([np.cos(outer).T, np.sin(outer).T], 1) * gain)
    last = np.concatenate([high, low], 0)
    twist = np.stack([np.cos(turn), np.sin(turn)]).astype(np.float32)
    return first, second, back, last, twist


def split(value):
    high = value.astype(bf16)
    low = (value - high.astype(f32)).astype(bf16)
    return high, low


def tails_kernel(q, k, v, out, near, sems):
    rows = q.shape[0]
    copies = [
        pltpu.make_async_copy(x.at[pl.ds(rows - TAIL, TAIL), :], near.at[which], sems.at[which])
        for which, x in enumerate((q, k, v))
    ]
    for copy in copies:
        copy.start()
    for which, copy in enumerate(copies):
        copy.wait()
        out[which] = near[which].astype(f32)[TAIL - EDGE :, :].astype(bf16)


ACROSS = (((1,), (1,)), ((), ()))


def fetch_kernel(
    here, q, k, v, filt, mine, w, taps_in, qs, ks, vs, gg, ft, wm, wo, taps, qb, kb, vb, fb, mb, pad, sems
):
    rows, width = q.shape
    half = w.shape[1] // 2
    me = here[0]
    w_mine = w.at[:, pl.ds(pl.multiple_of(me * half, half), half)]
    w_other = w.at[:, pl.ds(pl.multiple_of((1 - me) * half, half), half)]
    pairs = ((taps_in, taps), (q, qb), (k, kb), (v, vb), (filt, fb), (mine, mb), (w_mine, wm), (w_other, wo))
    copies = [pltpu.make_async_copy(src, dst, sems.at[i]) for i, (src, dst) in enumerate(pairs)]
    for copy in copies:
        copy.start()
    pad[0:EDGE, :] = jnp.zeros((EDGE, LANES), f32)
    copies[0].wait()
    for which, (buf, out) in enumerate(((qb, qs), (kb, ks), (vb, vs))):
        copies[1 + which].wait()
        for first in range(0, width, LANES):
            columns = slice(first, first + LANES)
            pad[EDGE : EDGE + rows, :] = buf[:, columns].astype(f32)
            total = taps[which, 0:1, columns] * pad[EDGE : EDGE + rows, :]
            for shift in range(1, taps.shape[1]):
                moved = pad[EDGE - shift : EDGE - shift + rows, :]
                total = total + taps[which, shift : shift + 1, columns] * moved
            out[:, columns] = total
    copies[4].wait()
    for first in range(0, width, WIDE):
        ft[first : first + WIDE, :] = fb[:, first : first + WIDE].T
    copies[5].wait()
    copies[6].wait()
    for first in range(0, width, WIDE):
        part = slice(first, first + WIDE)
        gg[:, part] = lax.dot_general(mb[...], wm[part, :], ACROSS, preferred_element_type=f32)
    copies[7].wait()


def prepare_kernel(halo, taps, qs_in, ks_in, vs_in, gg_in, ft, other, wo, send, qs, ks, vs, gg, pad):
    rows, width = gg.shape
    parts, lines, _ = send.shape
    group = lines // 3
    pad[EDGE : 2 * EDGE, :] = jnp.zeros((EDGE, WIDE), f32)
    for first in range(0, width, WIDE):
        part = slice(first, first + WIDE)
        grad = gg_in[:, part] + lax.dot_general(other[...], wo[part, :], ACROSS, preferred_element_type=f32)
        gg[:, part] = grad
        shorts = []
        for which, (before, after) in enumerate(((qs_in, qs), (ks_in, ks), (vs_in, vs))):
            pad[0:EDGE, :] = halo[which, :, part].astype(f32)
            top = before[0:EDGE, part]
            for shift in range(1, taps.shape[1]):
                top = top + taps[which, shift : shift + 1, part] * pad[EDGE - shift : 2 * EDGE - shift, :]
            value = jnp.concatenate([top, before[EDGE:, part]], 0)
            after[0:EDGE, part] = top
            shorts.append(value)
        mixed = (shorts[1] * shorts[2]).T
        grad_long = (grad * shorts[0]).T
        turned = [field.reshape(WIDE // group, group, rows) for field in (mixed, ft[part, :], grad_long)]
        send[first // group : (first + WIDE) // group] = jnp.concatenate(turned, axis=1).astype(bf16)


BATCH = 4


def spectral_kernel(x, first, second, back, last, twist, out, buf):
    parts, lines, rows = x.shape
    group = lines // 3
    buf[...] = x[...].astype(f32).reshape(parts * lines, rows)
    cos, sin = twist[0], twist[1]

    def dot(left, right):
        return jnp.dot(left, right, preferred_element_type=f32)

    def wide(value, table):
        high, low = split(value)
        count = value.shape[0]
        both = dot(jnp.concatenate([high, low], 0), table[0])
        return both[:count] + both[count:] + dot(high, table[1])

    def spot(f, c):
        return pl.ds(f * group + c, parts, stride=lines)

    for base in range(0, group, BATCH):
        lanes = range(base, min(base + BATCH, group))
        turned = []
        for c in lanes:
            field = jnp.concatenate([buf[spot(f, c), :] for f in range(3)], 1).astype(bf16)
            half = dot(first[...], jnp.concatenate([field, field], 0))
            for f in range(3):
                re = half[:parts, f * rows : (f + 1) * rows]
                im = half[parts:, f * rows : (f + 1) * rows]
                turned.append(jnp.concatenate([re * cos - im * sin, re * sin + im * cos], 1))
        spec = wide(jnp.concatenate(turned, 0), second)
        solved = []
        for i in range(len(lanes)):
            (xr, xi), (kr, ki), (gr, gi) = [
                (spec[f * parts : (f + 1) * parts, :rows], spec[f * parts : (f + 1) * parts, rows:])
                for f in range(3 * i, 3 * i + 3)
            ]
            solved.append(jnp.concatenate([xr * kr - xi * ki, xr * ki + xi * kr], 1))
            solved.append(jnp.concatenate([kr * gr + ki * gi, kr * gi - ki * gr], 1))
            solved.append(jnp.concatenate([xr * gr + xi * gi, xr * gi - xi * gr], 1))
        part = wide(jnp.concatenate(solved, 0), back)
        turned = []
        for f in range(3 * len(lanes)):
            re = part[f * parts : (f + 1) * parts, :rows]
            im = part[f * parts : (f + 1) * parts, rows:]
            turned.append(jnp.concatenate([re * cos + im * sin, im * cos - re * sin], 0))
        high, low = split(jnp.concatenate(turned, 1))
        both = dot(last[...], high)
        result = both[:parts] + both[parts:] + dot(last[:parts, :], low)
        for i, c in enumerate(lanes):
            for f in range(3):
                place = (3 * i + f) * rows
                buf[spot(f, c), :] = result[:, place : place + rows]
    out[...] = buf[...].reshape(parts, lines, rows).astype(bf16)


def gate_kernel(landed, qs, ks, vs, gg, wo, gq, gk, gv, heads, gated, other):
    rows, width = qs.shape
    parts, lines, _ = landed.shape
    group = lines // 3
    for first in range(0, width, WIDE):
        part = slice(first, first + WIDE)
        values = landed[first // group : (first + WIDE) // group].astype(f32)
        long_out, grad_mixed = [
            values[:, f * group : (f + 1) * group, :].reshape(WIDE, rows).T for f in range(2)
        ]
        gated[:, part] = (qs[:, part] * long_out).astype(bf16)
        for which, (to, value) in enumerate(
            (
                (gq, gg[:, part] * long_out),
                (gk, grad_mixed * vs[:, part]),
                (gv, grad_mixed * ks[:, part]),
            )
        ):
            to[:, part] = value
            heads[which, :, part] = value[:EDGE, :].astype(bf16)
    for first in range(0, width, WIDE):
        part = slice(first, first + WIDE)
        other[:, part] = jnp.dot(gated[...], wo[:, part], preferred_element_type=f32)


def project_kernel(
    landed, gated, wm, gq, gk, gv, taps, gf, mine, ends, oq, ok, ov, pad, turned, rounded, sems
):
    rows, width = gated.shape
    parts, lines, _ = landed.shape
    group = lines // 3
    for first in range(0, width, WIDE):
        part = slice(first, first + WIDE)
        values = landed[first // group : (first + WIDE) // group].astype(f32)
        turned[:, part] = values[:, 2 * group :, :].reshape(WIDE, rows).T
    copies = [pltpu.make_async_copy(turned, gf, sems.at[3])]
    copies[0].start()
    pad[rows : rows + EDGE, :] = jnp.zeros((EDGE, LANES), f32)
    for which, (value, to) in enumerate(((gq, oq), (gk, ok), (gv, ov))):
        for first in range(0, width, LANES):
            part = slice(first, first + LANES)
            pad[0:rows, :] = value[:, part]
            total = taps[which, 0:1, part] * value[:, part]
            for shift in range(1, taps.shape[1]):
                total = total + taps[which, shift : shift + 1, part] * pad[shift : shift + rows, :]
            rounded[which, :, part] = total.astype(bf16)
            ends[which, :, part] = total[rows - TAIL :, :]
        copy = pltpu.make_async_copy(rounded.at[which], to, sems.at[which])
        copy.start()
        copies.append(copy)
    for first in range(0, width, WIDE):
        part = slice(first, first + WIDE)
        mine[:, part] = jnp.dot(gated[...], wm[:, part], preferred_element_type=f32)
    for copy in copies:
        copy.wait()


def close_kernel(
    ends, after, taps, mine, other, near_q, near_k, near_v, block_out, oq, ok, ov, pad, tail, total, sems
):
    rows, width = mine.shape
    total[...] = (mine[...] + other[...]).astype(bf16)
    copies = [pltpu.make_async_copy(total, block_out, sems.at[3])]
    copies[0].start()
    pad[0:EDGE, :] = jnp.zeros((EDGE, width), f32)
    for which, to in enumerate((oq, ok, ov)):
        pad[EDGE : 2 * EDGE, :] = after[which].astype(f32)
        end = ends[which, TAIL - EDGE :, :]
        for shift in range(1, taps.shape[1]):
            end = end + taps[which, shift : shift + 1, :] * pad[shift : shift + EDGE, :]
        tail[which] = jnp.concatenate([ends[which, : TAIL - EDGE, :], end], 0).astype(bf16)
        copy = pltpu.make_async_copy(tail.at[which], to.at[pl.ds(rows - TAIL, TAIL), :], sems.at[which])
        copy.start()
        copies.append(copy)
    for copy in copies:
        copy.wait()


def on_device(query_in, key_in, value_in, taps, long_filter, out_weight, out_grad):
    rows, width = query_in.shape
    parts = lax.axis_size("ctx")
    seq_total = parts * rows
    group = width // parts
    lines = 3 * group
    outs = out_weight.shape[1]
    here = lax.axis_index("ch").astype(jnp.int32).reshape(1)
    gain = 1.0 / math.sqrt(seq_total) / seq_total
    swap = [(0, 1), (1, 0)]
    order = ring_order(parts)

    params = pltpu.CompilerParams(vmem_limit_bytes=VMEM_LIMIT)
    vmem = pl.BlockSpec(memory_space=pltpu.VMEM)
    hbm = pl.BlockSpec(memory_space=pltpu.HBM)
    smem = pl.BlockSpec(memory_space=pltpu.SMEM)
    flat = jax.ShapeDtypeStruct((rows, width), f32)
    half = jax.ShapeDtypeStruct((rows, width), bf16)
    fields = jax.ShapeDtypeStruct((parts, lines, rows), bf16)
    edges = jax.ShapeDtypeStruct((3, EDGE, width), bf16)
    weights = jax.ShapeDtypeStruct((width, outs // 2), bf16)
    cost = pl.CostEstimate(flops=2 * rows * width * outs, bytes_accessed=8 * 2**20, transcendentals=0)

    grad_other = lax.ppermute(out_grad, "ch", swap)
    far = [
        pltpu.with_memory_space_constraint(x, pltpu.HBM)
        for x in (query_in, key_in, value_in, long_filter, out_grad, out_weight, taps)
    ]
    with jax.named_scope("tails"):
        tails = pl.pallas_call(
            tails_kernel,
            in_specs=[hbm] * 3,
            out_specs=vmem,
            out_shape=edges,
            scratch_shapes=[pltpu.VMEM((3, TAIL, width), bf16), pltpu.SemaphoreType.DMA((3,))],
            compiler_params=params,
        )(*far[:3])
    halo = shifted(tails, "ctx", 1)

    with jax.named_scope("fetch"):
        qs, ks, vs, gg, ft, wm, wo, taps_near = pl.pallas_call(
            fetch_kernel,
            in_specs=[smem] + [hbm] * 7,
            out_specs=[vmem] * 8,
            out_shape=[
                flat,
                flat,
                flat,
                flat,
                jax.ShapeDtypeStruct((width, rows), f32),
                weights,
                weights,
                jax.ShapeDtypeStruct(taps.shape, f32),
            ],
            scratch_shapes=[
                pltpu.VMEM((rows, width), bf16),
                pltpu.VMEM((rows, width), bf16),
                pltpu.VMEM((rows, width), bf16),
                pltpu.VMEM((rows, width), f32),
                pltpu.VMEM((rows, width), bf16),
                pltpu.VMEM((rows + EDGE, LANES), f32),
                pltpu.SemaphoreType.DMA((8,)),
            ],
            compiler_params=params,
            cost_estimate=cost,
        )(here, *far)

    with jax.named_scope("prepare"):
        send, qs, ks, vs, gg = pl.pallas_call(
            prepare_kernel,
            in_specs=[vmem] * 9,
            out_specs=[vmem] * 5,
            out_shape=[fields, flat, flat, flat, flat],
            input_output_aliases={2: 1, 3: 2, 4: 3},
            scratch_shapes=[pltpu.VMEM((2 * EDGE, WIDE), f32)],
            compiler_params=params,
        )(halo, taps_near, qs, ks, vs, gg, ft, grad_other, wo)

    arrived = lax.all_to_all(
        send, "ctx", split_axis=0, concat_axis=0, tiled=True, axis_index_groups=[order]
    )

    with jax.named_scope("spectral"):
        solved = pl.pallas_call(
            spectral_kernel,
            out_shape=fields,
            scratch_shapes=[pltpu.VMEM((parts * lines, rows), f32)],
            compiler_params=params,
        )(arrived, *tables(parts, rows, gain, order))

    landed = lax.all_to_all(
        solved, "ctx", split_axis=0, concat_axis=0, tiled=True, axis_index_groups=[order]
    )

    with jax.named_scope("gate"):
        gq, gk, gv, heads, gated, other = pl.pallas_call(
            gate_kernel,
            in_specs=[vmem] * 6,
            out_specs=[vmem] * 6,
            out_shape=[flat, flat, flat, edges, half, flat],
            compiler_params=params,
        )(landed, qs, ks, vs, gg, wo)

    after = shifted(heads, "ctx", -1)
    theirs = lax.ppermute(other, "ch", swap)

    with jax.named_scope("project"):
        grad_filter, mine, ends, oq, ok, ov = pl.pallas_call(
            project_kernel,
            in_specs=[vmem] * 7,
            out_specs=[hbm, vmem, vmem, hbm, hbm, hbm],
            out_shape=[flat, flat, jax.ShapeDtypeStruct((3, TAIL, width), f32), half, half, half],
            scratch_shapes=[
                pltpu.VMEM((rows + EDGE, LANES), f32),
                pltpu.VMEM((rows, width), f32),
                pltpu.VMEM((3, rows, width), bf16),
                pltpu.SemaphoreType.DMA((4,)),
            ],
            compiler_params=params,
            cost_estimate=cost,
        )(landed, gated, wm, gq, gk, gv, taps_near)

    with jax.named_scope("close"):
        begun = [pltpu.with_memory_space_constraint(x, pltpu.HBM) for x in (oq, ok, ov)]
        block_out, grad_query, grad_key, grad_value = pl.pallas_call(
            close_kernel,
            in_specs=[vmem] * 5 + [hbm] * 3,
            out_specs=[hbm] * 4,
            out_shape=[half] * 4,
            input_output_aliases={5: 1, 6: 2, 7: 3},
            scratch_shapes=[
                pltpu.VMEM((2 * EDGE, width), f32),
                pltpu.VMEM((3, TAIL, width), bf16),
                pltpu.VMEM((rows, width), bf16),
                pltpu.SemaphoreType.DMA((4,)),
            ],
            compiler_params=params,
        )(ends, after, taps_near, mine, theirs, *begun)
    return (block_out, grad_query, grad_key, grad_value, grad_filter)


def solution(mesh):
    return jax.shard_map(
        on_device,
        mesh=mesh,
        in_specs=(
            P("ctx", "ch"),
            P("ctx", "ch"),
            P("ctx", "ch"),
            P(None, None, "ch"),
            P("ctx", "ch"),
            P("ch", None),
            P("ctx", "ch"),
        ),
        out_specs=(P("ctx", "ch"), P("ctx", "ch"), P("ctx", "ch"), P("ctx", "ch"), P("ctx", "ch")),
        check_vma=False,
    )
```
